256 devices in a mesh: mem: 8 (over z), reg: 32 (over y, x, core).
Axes of the slice: x: 4, y: 4, z: 8, core: 2. Of those that a mesh axis runs over, the one named last changes fastest.
Arguments:
- background: bfloat16 [32, 32, 256, 640], P('reg', None, 'mem'), may hold values from -6 to 6
- obs_ensemble: bfloat16 [32, 32, 2048, 256], P('reg', 'mem'), may hold values from -180 to 180
- innovation: bfloat16 [32, 32, 2048], P('reg', 'mem'), may hold values from -8 to 8
- obs_precision: bfloat16 [32, 32, 2048], P('reg', 'mem'), may hold values from 0.25 to 4
- taper_weight: bfloat16 [32, 32, 5, 2048], P('reg', 'mem'), may hold values from 0.049804688 to 1
- obs_count: int32 [32, 32], P('reg', 'mem'), may hold values from 256 to 2048, as said below
Outputs:
- analysis: bfloat16 [32, 32, 256, 640], P('reg', None, 'mem')
The draws below stay inside these ranges and needn't reach their ends.
Inputs may be any that keep to these rules, and one draw needn't show every extreme that they name: Slots 0 to obs_count - 1 of a patch hold its observations; in every draw some patch has all 2048 slots filled.
All inputs are finite; a program needn't handle non-finite values. Where the reference program divides by a largest or mean magnitude, that divisor is 1e-20 or more.
Results may differ from the reference program's by a relative error of at most 0.0063.
Values may be sent and summed in bfloat16 or wider, within the bound.
No kernel may reach another device: no remote copies, remote signals or barrier semaphores. Data moves between devices by JAX's collectives and lax.ppermute only.
A program may use at most 128 MiB of HBM per device.

```python
import math
import jax
import jax.numpy as jnp
from jax import lax

K = 256
OBS_CAP = 2048
ITERS = 12
REGIONS = 32
PCOLS = 32
ROWS = 640


def draw_obs_ensemble(key, part):
    key = jax.random.fold_in(key, 5)
    first, second = jax.random.split(key, 2)
    member_scale = jnp.exp(jax.random.uniform(first, (REGIONS, PCOLS, 1, K), jnp.float32, math.log(0.3), math.log(30.0)))
    base = jnp.clip(jax.random.normal(second, (REGIONS, PCOLS, OBS_CAP, K), jnp.float32), -6.0, 6.0)
    return (base * member_scale).astype(jnp.bfloat16)


def draw_obs_count(key, part):
    key = jax.random.fold_in(key, 11)
    first, second = jax.random.split(key)
    divisor = jax.random.randint(first, (REGIONS * PCOLS,), 1, 9, dtype=jnp.int32)
    counts = (OBS_CAP // divisor).astype(jnp.int32)
    chosen = jax.random.randint(second, (), 0, REGIONS * PCOLS, dtype=jnp.int32)
    counts = counts.at[chosen].set(OBS_CAP)
    return counts.reshape(REGIONS, PCOLS).astype(jnp.int32)


def level_of(key, shape, shards, low, high):
    factor_of, own = 1.0, jax.random.fold_in(key, 6)
    for position, blocks in shards:
        draws = jnp.exp(jax.random.uniform(jax.random.fold_in(own, position), (blocks,), jnp.float32, low / len(shards), high / len(shards)))
        factor_of = factor_of * jnp.repeat(draws, shape[position] // blocks).reshape([-1 if axis == position else 1 for axis in range(len(shape))])
    return factor_of


def scatter_about(own_key, dims, scale, reach, pieces=(), held_as=jnp.bfloat16):
    level = level_of(own_key, dims, pieces, -0.22, 0.18) if pieces else 1.0
    entries = jax.random.normal(own_key, dims, jnp.float32) * scale * level
    return jnp.minimum(jnp.maximum(entries, -reach), reach).astype(held_as)


def setup_inputs(seed: int = 0) -> dict:
    keys = jax.random.split(jax.random.key(seed), 7)
    return {
        "background": scatter_about(keys[0], (REGIONS, PCOLS, K, ROWS), 1.0, 6.0, ((0, 32), (2, 8))),
        "obs_ensemble": draw_obs_ensemble(jax.random.fold_in(keys[6], 71), 0),
        "innovation": scatter_about(keys[2], (REGIONS, PCOLS, OBS_CAP), 2.0, 8.0, ((0, 32), (1, 8))),
        "obs_precision": jnp.clip(jnp.exp(math.log(4.0) - 2.7725887 * jax.random.uniform(keys[3], (REGIONS, PCOLS, OBS_CAP), jnp.float32) ** level_of(keys[3], (REGIONS, PCOLS, OBS_CAP), ((0, 32), (1, 8)), -0.2, 0.2)), 0.25, 4.0).astype(jnp.bfloat16),
        "taper_weight": jnp.clip(0.049804688 + 0.9501953 * jax.random.uniform(keys[4], (REGIONS, PCOLS, 5, OBS_CAP), jnp.float32) ** level_of(keys[4], (REGIONS, PCOLS, 5, OBS_CAP), ((0, 32), (1, 8)), -0.2, 0.2), 0.049804688, 1.0).astype(jnp.bfloat16),
        "obs_count": draw_obs_count(jax.random.fold_in(keys[6], 71), 0),
    }


def square_root_weights(gram, drive):
    ident = jnp.eye(K, dtype=jnp.float32)
    system = gram + float(K - 1) * ident
    bound = lax.optimization_barrier(jnp.max(lax.optimization_barrier(jnp.sum(jnp.abs(system), axis=2)), axis=1))
    root = system / bound[:, None, None]
    inverse = jnp.broadcast_to(ident, system.shape)

    def sweep(step_index, carry):
        root, inverse = carry
        step = 1.5 * ident - 0.5 * jnp.einsum('pij,pjk->pik', inverse, root, precision=lax.Precision.HIGHEST)
        root = jnp.einsum('pij,pjk->pik', root, step, precision=lax.Precision.HIGHEST)
        inverse = jnp.einsum('pij,pjk->pik', step, inverse, precision=lax.Precision.HIGHEST)
        return (root, inverse)
    root, inverse = lax.fori_loop(0, ITERS, sweep, (root, inverse))
    half = inverse / jnp.sqrt(bound)[:, None, None]
    inner = jnp.einsum('pkl,pl->pk', half, drive, precision=lax.Precision.HIGHEST)
    mean_weight = jnp.einsum('pkl,pl->pk', half, inner, precision=lax.Precision.HIGHEST)
    transform = jnp.sqrt(float(K - 1)) * half + mean_weight[:, :, None]
    return transform.astype(jnp.bfloat16)

def reference(background, obs_ensemble, innovation, obs_precision, taper_weight, obs_count):
    slots = jnp.arange(OBS_CAP, dtype=jnp.int32)
    valid = slots[None, None, :] < obs_count[:, :, None]
    weight = jnp.where(valid[:, :, None, :], obs_precision.astype(jnp.float32)[:, :, None, :] * taper_weight.astype(jnp.float32), 0.0)

    def grams(row, side_index):
        ens = lax.dynamic_index_in_dim(obs_ensemble, row, 0, keepdims=False)
        innov = lax.dynamic_index_in_dim(innovation, row, 0, keepdims=False)
        wts = lax.dynamic_index_in_dim(weight, row, 0, keepdims=False)[:, side_index, :]
        scaled = (wts[:, :, None] * ens.astype(jnp.float32)).astype(jnp.bfloat16)
        gram = jnp.einsum('pok,pol->pkl', scaled.astype(jnp.float32), ens.astype(jnp.float32))
        drive = jnp.einsum('pok,po->pk', scaled.astype(jnp.float32), innov.astype(jnp.float32))
        return (gram, drive)

    def analyse(row):
        above = ((row - 1) % REGIONS).astype(jnp.int32)
        below = ((row + 1) % REGIONS).astype(jnp.int32)
        g_own, d_own = grams(row, 0)
        g_up, d_up = grams(above, 1)
        g_down, d_down = grams(below, 2)
        g_next, d_next = grams(row, 3)
        g_prev, d_prev = grams(row, 4)
        gram = g_own + g_up + g_down + jnp.roll(g_next, 1, axis=0) + jnp.roll(g_prev, -1, axis=0)
        drive = d_own + d_up + d_down + jnp.roll(d_next, 1, axis=0) + jnp.roll(d_prev, -1, axis=0)
        transform = square_root_weights(gram, drive)
        states = lax.dynamic_index_in_dim(background, row, 0, keepdims=False).astype(jnp.float32)
        mean_state = lax.optimization_barrier(jnp.mean(states, axis=1, keepdims=True))
        perturbation = (states - mean_state).astype(jnp.bfloat16)
        result = mean_state + jnp.einsum('pki,pkr->pir', transform.astype(jnp.float32), perturbation.astype(jnp.float32))
        return result.astype(jnp.bfloat16)
    return lax.map(analyse, jnp.arange(REGIONS, dtype=jnp.int32))
```

```python
import jax
import jax.numpy as jnp
from jax import lax
from jax.experimental import pallas as pl
from jax.experimental.pallas import tpu as pltpu
from jax.sharding import PartitionSpec as P

F32 = jnp.float32
BF16 = jnp.bfloat16
ITERS = 12
PATCHES = 4
K = 256
SLOTS = 2048
CHUNK = 512
PEERS = 8
EXT = K + 8
VMEM = pl.BlockSpec(memory_space=pltpu.VMEM)
SMEM = pl.BlockSpec(memory_space=pltpu.SMEM)
PARAMS = pltpu.CompilerParams(vmem_limit_bytes=56 << 20)


def dot(a, b):
    return jnp.dot(a, b, preferred_element_type=F32)


def split(x):
    high = x.astype(BF16)
    return high, (x - high.astype(F32)).astype(BF16)


def dot_split(a, b):
    return dot(a[0], b[0]) + (dot(a[0], b[1]) + dot(a[1], b[0]))


def pick_row(ref, p):
    patch = lax.broadcasted_iota(jnp.int32, (PATCHES, SLOTS), 0)
    return jnp.sum(jnp.where(patch == p, ref[0].astype(F32), 0.0), axis=0, keepdims=True)


def slot_weights(p, count_ref, prec_ref, taper_ref):
    slot = lax.broadcasted_iota(jnp.int32, (1, SLOTS), 1)
    prec = jnp.where(slot < count_ref[p], pick_row(prec_ref, p), 0.0)
    return prec * taper_ref[0, p].astype(F32)


def weighted_grams(ens_ref, weights, innov, sides, add):
    rows = jnp.concatenate([weights[d : d + 1] for d in sides], axis=0)
    driven = split(rows * innov)
    for c in range(SLOTS // CHUNK):
        part = slice(c * CHUNK, (c + 1) * CHUNK)
        ens = ens_ref[0, 0, part, :]
        flipped = ens.T.astype(F32)
        drives = dot(driven[0][:, part], ens) + dot(driven[1][:, part], ens)
        for i, d in enumerate(sides):
            scaled = (flipped * weights[d : d + 1, part]).astype(BF16)
            add(c, d, dot(scaled, ens), drives[i : i + 1])


def sent_kernel(count_ref, ens_ref, innov_ref, prec_ref, taper_ref, above_ref, below_ref, next_ref, prev_ref):
    p = pl.program_id(0)
    weights = slot_weights(p, count_ref, prec_ref, taper_ref)
    innov = pick_row(innov_ref, p)

    def adder(targets):
        def add(c, d, gram, drive):
            ref = targets[d]
            if c == 0:
                ref[0, 0:K, :] = gram
                ref[0, K : K + 1, :] = drive
                ref[0, K + 1 : EXT, :] = jnp.zeros((EXT - K - 1, K), F32)
            else:
                ref[0, 0:K, :] += gram
                ref[0, K : K + 1, :] += drive

        return add

    @pl.when(p == 0)
    def _():
        weighted_grams(ens_ref, weights, innov, (1, 2, 4), adder({1: above_ref, 2: below_ref, 4: prev_ref}))

    @pl.when((p > 0) & (p < PATCHES - 1))
    def _():
        weighted_grams(ens_ref, weights, innov, (1, 2), adder({1: above_ref, 2: below_ref}))

    @pl.when(p == PATCHES - 1)
    def _():
        weighted_grams(ens_ref, weights, innov, (1, 2, 3), adder({1: above_ref, 2: below_ref, 3: next_ref}))


def kept_kernel(count_ref, ens_ref, innov_ref, prec_ref, taper_ref, own_ref):
    p = pl.program_id(0)
    weights = slot_weights(p, count_ref, prec_ref, taper_ref)
    innov = pick_row(innov_ref, p)

    @pl.when(p == 0)
    def _():
        own_ref[...] = jnp.zeros_like(own_ref)

    shift = {0: 0, 3: 1, 4: -1}

    def add(c, d, gram, drive):
        to = p + shift[d]
        own_ref[to, 0:K, :] += gram
        own_ref[to, K : K + 1, :] += drive

    @pl.when(p == 0)
    def _():
        weighted_grams(ens_ref, weights, innov, (0, 3), add)

    @pl.when((p > 0) & (p < PATCHES - 1))
    def _():
        weighted_grams(ens_ref, weights, innov, (0, 3, 4), add)

    @pl.when(p == PATCHES - 1)
    def _():
        weighted_grams(ens_ref, weights, innov, (0, 4), add)


def gram_specs():
    return [
        SMEM,
        pl.BlockSpec((1, 1, SLOTS, K), lambda p: (0, p, 0, 0)),
        pl.BlockSpec((1, PATCHES, SLOTS), lambda p: (0, 0, 0)),
        pl.BlockSpec((1, PATCHES, SLOTS), lambda p: (0, 0, 0)),
        pl.BlockSpec((1, PATCHES, 5, SLOTS), lambda p: (0, 0, 0, 0)),
    ]


def cost(grams):
    return pl.CostEstimate(flops=grams * 2 * K * K * SLOTS, bytes_accessed=PATCHES * SLOTS * K * 2, transcendentals=0)


def sent_grams(*args):
    full = jax.ShapeDtypeStruct((PATCHES, EXT, K), F32)
    one = jax.ShapeDtypeStruct((1, EXT, K), F32)
    return pl.pallas_call(
        sent_kernel,
        grid=(PATCHES,),
        in_specs=gram_specs(),
        out_specs=[pl.BlockSpec((1, EXT, K), lambda p: (p, 0, 0))] * 2 + [pl.BlockSpec((1, EXT, K), lambda p: (0, 0, 0))] * 2,
        out_shape=[full, full, one, one],
        compiler_params=PARAMS,
        cost_estimate=cost(10),
        name="sent_grams",
    )(*args)


def kept_grams(*args):
    return pl.pallas_call(
        kept_kernel,
        grid=(PATCHES,),
        in_specs=gram_specs(),
        out_specs=pl.BlockSpec((PATCHES, EXT, K), lambda p: (0, 0, 0)),
        out_shape=jax.ShapeDtypeStruct((PATCHES, EXT, K), F32),
        compiler_params=PARAMS,
        cost_estimate=cost(10),
        name="kept_grams",
    )(*args)


def root_kernel(own_ref, above_ref, below_ref, next_ref, prev_ref, out_ref, y_ref, z_ref, bound_ref):
    row = lax.broadcasted_iota(jnp.int32, (K, K), 0)
    col = lax.broadcasted_iota(jnp.int32, (K, K), 1)
    ident = jnp.where(row == col, 1.0, 0.0).astype(F32)

    def total(p, part):
        value = own_ref[p, part, :] + above_ref[p, part, :] + below_ref[p, part, :]
        if p == 0:
            value = value + next_ref[0, part, :]
        if p == PATCHES - 1:
            value = value + prev_ref[0, part, :]
        return value

    for p in range(PATCHES):
        system = total(p, slice(0, K)) + float(K - 1) * ident
        sums = jnp.sum(jnp.abs(system), axis=0, keepdims=True)
        bound = jnp.max(sums, axis=1, keepdims=True)
        bound_ref[p] = jnp.broadcast_to(bound, (8, 128))
        root = system / bound
        step = 1.5 * ident - 0.5 * root
        y_ref[p] = dot_split(split(root), split(step))
        z_ref[p] = step

    def sweep(index, carry):
        for p in range(PATCHES):
            y = split(y_ref[p])
            z = split(z_ref[p])
            step = split(1.5 * ident - 0.5 * dot_split(z, y))
            y_ref[p] = dot_split(y, step)
            z_ref[p] = dot_split(step, z)
        return carry

    lax.fori_loop(0, ITERS - 1, sweep, 0)
    for p in range(PATCHES):
        half = z_ref[p] / jnp.sqrt(bound_ref[p, 0:1, 0:1])
        drive = total(p, slice(K, K + 1))
        inner = jnp.sum(half * drive, axis=1, keepdims=True)
        mean_weight = jnp.sum(half * inner, axis=0, keepdims=True)
        out_ref[p] = (jnp.sqrt(float(K - 1)) * half + mean_weight).astype(BF16)


def root_weights(*args):
    return pl.pallas_call(
        root_kernel,
        in_specs=[VMEM] * 5,
        out_specs=VMEM,
        out_shape=jax.ShapeDtypeStruct((PATCHES, K, K), BF16),
        scratch_shapes=[
            pltpu.VMEM((PATCHES, K, K), F32),
            pltpu.VMEM((PATCHES, K, K), F32),
            pltpu.VMEM((PATCHES, 8, 128), F32),
        ],
        compiler_params=PARAMS,
        cost_estimate=pl.CostEstimate(flops=PATCHES * 99 * 2 * K**3, bytes_accessed=4 << 20, transcendentals=0),
        name="root_weights",
    )(*args)


def apply_kernel(flipped_ref, states_ref, out_ref):
    rows = states_ref.shape[3]
    states = states_ref[:, 0].reshape(K, rows).astype(F32)
    mean = jnp.sum(states, axis=0, keepdims=True) * (1.0 / K)
    pert = (states - mean).astype(BF16)
    result = mean + dot(flipped_ref[0], pert)
    out_ref[:, 0] = result.astype(BF16).reshape(PEERS, K // PEERS, rows)


def apply_weights(flipped, states):
    rows = states.shape[3]
    block = pl.BlockSpec((PEERS, 1, K // PEERS, rows), lambda p: (0, p, 0, 0))
    return pl.pallas_call(
        apply_kernel,
        grid=(PATCHES,),
        in_specs=[pl.BlockSpec((1, K, K), lambda p: (p, 0, 0)), block],
        out_specs=block,
        out_shape=jax.ShapeDtypeStruct(states.shape, BF16),
        compiler_params=PARAMS,
        cost_estimate=pl.CostEstimate(flops=PATCHES * 2 * K * K * rows, bytes_accessed=4 << 20, transcendentals=0),
        name="apply_weights",
    )(flipped, states)


def swap(value):
    return lax.all_to_all(value, "mem", split_axis=0, concat_axis=0, tiled=True)


def shift(value, axis, by):
    peers = lax.axis_size(axis)
    return lax.ppermute(value, axis, [(i, (i + by) % peers) for i in range(peers)])


def body(background, obs_ensemble, innovation, obs_precision, taper_weight, obs_count):
    rows = background.shape[3]
    states = swap(background.reshape(PEERS, PATCHES, K // PEERS, rows))
    obs = (obs_count.reshape(PATCHES), obs_ensemble, innovation, obs_precision, taper_weight)
    above, below, following, previous = sent_grams(*obs)
    above = shift(above, "reg", 1)
    below = shift(below, "reg", -1)
    following = shift(following, "mem", 1)
    previous = shift(previous, "mem", -1)
    own = kept_grams(*obs)
    flipped = root_weights(own, above, below, following, previous)
    analysis = swap(apply_weights(flipped, states))
    return analysis.reshape(1, PEERS * PATCHES, K // PEERS, rows)


def solution(mesh):
    in_specs = (
        P("reg", None, "mem", None),
        P("reg", "mem", None, None),
        P("reg", "mem", None),
        P("reg", "mem", None),
        P("reg", "mem", None, None),
        P("reg", "mem"),
    )
    out_specs = P("reg", None, "mem", None)
    return jax.shard_map(body, mesh=mesh, in_specs=in_specs, out_specs=out_specs, check_vma=False)
```

```python
import functools
import jax
import jax.numpy as jnp
from jax import lax
from jax.experimental import pallas as pl
from jax.experimental.pallas import tpu as pltpu
from jax.sharding import PartitionSpec as P

F32 = jnp.float32
BF16 = jnp.bfloat16
ITERS = 12
ROOT_COST = 2 * 10**9
PATCHES = 4
SIDES = 5
K = 256
SLOTS = 2048
PEERS = 8
EXT = K + 8
VMEM = pl.BlockSpec(memory_space=pltpu.VMEM)
SMEM = pl.BlockSpec(memory_space=pltpu.SMEM)
ANY = pl.BlockSpec(memory_space=pl.ANY)
PARAMS = pltpu.CompilerParams(vmem_limit_bytes=24 << 20)
SMALL = pltpu.CompilerParams(vmem_limit_bytes=16 << 20)
COST = pl.CostEstimate(flops=1000, bytes_accessed=1000, transcendentals=0)


def dot(a, b):
    return jnp.dot(a, b, preferred_element_type=F32)


def split(x):
    high = x.astype(BF16)
    return high, (x - high.astype(F32)).astype(BF16)


def start_all(copies):
    for copy in copies:
        copy.start()


def pick_row(value, p):
    patch = lax.broadcasted_iota(jnp.int32, (PATCHES, SLOTS), 0)
    return jnp.sum(jnp.where(patch == p, value.astype(F32), 0.0), axis=0, keepdims=True)


def slot_weights(p, count_ref, prec_ref, taper_ref):
    slot = lax.broadcasted_iota(jnp.int32, (1, SLOTS), 1)
    prec = jnp.where(slot < count_ref[p], pick_row(prec_ref[0], p), 0.0)
    return [prec * pick_row(taper_ref[0, d], p) for d in range(SIDES)]


def weighted_grams(ens_ref, flipped_ref, rows, innov):
    flipped_ref[...] = ens_ref[0, 0].T
    driven = jnp.concatenate([row * innov for row in rows] + [jnp.zeros((8 - len(rows), SLOTS), F32)], axis=0)
    scaled = [(flipped_ref[...].astype(F32) * row).astype(BF16) for row in rows]
    both = dot(jnp.concatenate(scaled + list(split(driven)), axis=0), ens_ref[0, 0])
    n = len(rows) * K
    drives = both[n : n + 8] + both[n + 8 : n + 16]
    return [(both[i * K : (i + 1) * K], drives[i : i + 1]) for i in range(len(rows))]


def sent_kernel(count_ref, ens_ref, innov_ref, prec_ref, taper_ref, near_ref, far_ref, next_ref, prev_ref, flipped_ref):
    p = pl.program_id(0)
    even = lax.rem(lax.axis_index("reg"), 2) == 0
    weights = slot_weights(p, count_ref, prec_ref, taper_ref)
    sided = [jnp.where(even, weights[1], weights[2]), jnp.where(even, weights[2], weights[1])]
    innov = pick_row(innov_ref[0], p)

    def store(rows, refs):
        for (gram, drive), ref in zip(weighted_grams(ens_ref, flipped_ref, rows, innov), refs):
            ref[0, 0:K, :] = gram
            ref[0, K:EXT, :] = jnp.broadcast_to(drive, (EXT - K, K))

    @pl.when(p == 0)
    def _():
        store(sided + [weights[4]], (near_ref, far_ref, prev_ref))

    @pl.when((p > 0) & (p < PATCHES - 1))
    def _():
        store(sided, (near_ref, far_ref))

    @pl.when(p == PATCHES - 1)
    def _():
        store(sided + [weights[3]], (near_ref, far_ref, next_ref))


def kept_kernel(count_ref, ens_ref, innov_ref, prec_ref, taper_ref, own_ref, flipped_ref):
    p = pl.program_id(0)
    weights = slot_weights(p, count_ref, prec_ref, taper_ref)
    innov = pick_row(innov_ref[0], p)

    @pl.when(p == 0)
    def _():
        own_ref[...] = jnp.zeros_like(own_ref)

    def add(sides):
        pairs = weighted_grams(ens_ref, flipped_ref, [weights[d] for d in sides], innov)
        for d, (gram, drive) in zip(sides, pairs):
            to = p + {0: 0, 3: 1, 4: -1}[d]
            own_ref[to, 0:K, :] += gram
            own_ref[to, K : K + 1, :] += drive

    @pl.when(p == 0)
    def _():
        add((0, 3))

    @pl.when((p > 0) & (p < PATCHES - 1))
    def _():
        add((0, 3, 4))

    @pl.when(p == PATCHES - 1)
    def _():
        add((0, 4))


def gram_specs():
    return [
        SMEM,
        pl.BlockSpec((1, 1, SLOTS, K), lambda p: (0, p, 0, 0)),
        pl.BlockSpec((1, PATCHES, SLOTS), lambda p: (0, 0, 0)),
        pl.BlockSpec((1, PATCHES, SLOTS), lambda p: (0, 0, 0)),
        pl.BlockSpec((1, SIDES, PATCHES, SLOTS), lambda p: (0, 0, 0, 0)),
    ]


def sent_grams(*args):
    full = jax.ShapeDtypeStruct((PATCHES, EXT, K), F32)
    one = jax.ShapeDtypeStruct((1, EXT, K), F32)
    return pl.pallas_call(
        sent_kernel,
        grid=(PATCHES,),
        in_specs=gram_specs(),
        out_specs=[pl.BlockSpec((1, EXT, K), lambda p: (p, 0, 0))] * 2 + [pl.BlockSpec((1, EXT, K), lambda p: (0, 0, 0))] * 2,
        out_shape=[full, full, one, one],
        scratch_shapes=[pltpu.VMEM((K, SLOTS), BF16)],
        compiler_params=PARAMS,
        cost_estimate=COST,
        name="sent_grams",
    )(*args)


def kept_grams(*args):
    return pl.pallas_call(
        kept_kernel,
        grid=(PATCHES,),
        in_specs=gram_specs(),
        out_specs=pl.BlockSpec((PATCHES, EXT, K), lambda p: (0, 0, 0)),
        out_shape=jax.ShapeDtypeStruct((PATCHES, EXT, K), F32),
        scratch_shapes=[pltpu.VMEM((K, SLOTS), BF16)],
        compiler_params=PARAMS,
        cost_estimate=COST,
        name="kept_grams",
    )(*args)


def split_to(refs, p, x):
    refs[0][p], refs[1][p] = split(x)


def root_kernel(patches, *refs):
    edges = len(patches) > 0 and patches[0] == 0
    count = 5 if edges else 3
    sources, out_ref, held, rest = refs[:count], refs[count], refs[count + 1 : 2 * count + 1], refs[2 * count + 1 :]
    sems, yh, yl, zh, zl, sh, sl, diag_ref, scale_ref = rest
    y, z, s = (yh, yl), (zh, zl), (sh, sl)
    n = len(patches)
    copies = []
    for p in range(n):
        which = [0, 1, 2] + ([3 if p == 0 else 4] if edges else [])
        at = [patches[p]] * 3 + [0]
        copies.append(
            [pltpu.make_async_copy(sources[w].at[i], held[w].at[p if w < 3 else 0], sems.at[p, j]) for j, (w, i) in enumerate(zip(which, at))]
        )
        start_all(copies[p])
    row = lax.broadcasted_iota(jnp.int32, (K, K), 0)
    col = lax.broadcasted_iota(jnp.int32, (K, K), 1)
    diag_ref[...] = jnp.where(row == col, 1.5, 0.0).astype(F32)

    def total(p, part):
        value = held[0][p, part, :] + held[1][p, part, :] + held[2][p, part, :]
        return value + held[3 + p][0, part, :] if edges else value

    def product(a, b, p):
        ah, al, bh, bl = a[0][p], a[1][p], b[0][p], b[1][p]
        return dot(jnp.concatenate([ah, ah, al], axis=1), jnp.concatenate([bl, bh, bh], axis=0))

    def residual(p):
        split_to(s, p, diag_ref[...] - 0.5 * product(z, y, p))

    for p in range(n):
        for copy in copies[p]:
            copy.wait()
        system = total(p, slice(0, K)) + jnp.where(row == col, float(K - 1), 0.0)
        bound = jnp.max(jnp.sum(jnp.abs(system), axis=1, keepdims=True), axis=0, keepdims=True)
        scale_ref[p] = jnp.broadcast_to(1.0 / jnp.sqrt(bound), (8, K))
        root = system / bound
        split_to(y, p, root)
        split_to(z, p, diag_ref[...] - 0.5 * root)
    for p in range(n):
        split_to(y, p, product(y, z, p))

    def sweep(index, carry):
        for p in range(n):
            residual(p)
        for p in range(n):
            split_to(y, p, product(y, s, p))
            split_to(z, p, product(s, z, p))
        return carry

    lax.fori_loop(0, ITERS - 2, sweep, 0, unroll=2)
    for p in range(n):
        residual(p)
    for p in range(n):
        half = product(s, z, p) * scale_ref[p, 0:1, :]
        flipped = half.T
        inner = jnp.sum(half * total(p, slice(K, K + 1)), axis=1, keepdims=True)
        mean_weight = jnp.sum(flipped * inner, axis=0, keepdims=True)
        out_ref[p] = (jnp.sqrt(float(K - 1)) * flipped + mean_weight).astype(BF16)


def root_weights(patches, *args):
    n = len(patches)
    piece = pltpu.VMEM((n, K, K), BF16)
    full, one = pltpu.VMEM((n, EXT, K), F32), pltpu.VMEM((1, EXT, K), F32)
    return pl.pallas_call(
        functools.partial(root_kernel, patches),
        in_specs=[ANY] * len(args),
        out_specs=VMEM,
        out_shape=jax.ShapeDtypeStruct((n, K, K), BF16),
        scratch_shapes=([full] * 3 + [one] * 2)[: len(args)]
        + [pltpu.SemaphoreType.DMA((n, 4))]
        + [piece] * 6
        + [pltpu.VMEM((K, K), F32), pltpu.VMEM((n, 8, K), F32)],
        compiler_params=PARAMS,
        cost_estimate=pl.CostEstimate(flops=ROOT_COST, bytes_accessed=1000, transcendentals=0),
        name="root_weights",
    )(*args)


def apply_kernel(inner_ref, outer_ref, states, c0, c2, c6, c1, c7, c4, states_s, result_s, sems):
    rows = states_s.shape[3]
    me = lax.axis_index("mem")
    copies = [pltpu.make_async_copy(states.at[:, p], states_s.at[:, p], sems.at[p]) for p in range(PATCHES)]
    start_all(copies)
    flipped = (outer_ref[0], inner_ref[0], inner_ref[1], outer_ref[1])
    for p in range(PATCHES):
        copies[p].wait()
        value = states_s[:, p].reshape(K, rows).astype(F32)
        mean = jnp.sum(value, axis=0, keepdims=True) * (1.0 / K)
        result = mean + dot(flipped[p], (value - mean).astype(BF16))
        result_s[:, p] = result.astype(BF16).reshape(PEERS, K // PEERS, rows)

    def away(places):
        return result_s[lax.rem(me + places, PEERS)]

    c0[...] = away(0)
    c2[0:PATCHES] = away(2)
    c2[PATCHES:] = away(3)
    c6[0:PATCHES] = away(6)
    c6[PATCHES:] = away(5)
    c1[...] = away(1)
    c7[...] = away(7)
    c4[...] = away(4)


def apply_weights(inner, outer, states):
    block = states.shape[1:]
    twice = (2 * PATCHES,) + block[1:]
    return pl.pallas_call(
        apply_kernel,
        in_specs=[VMEM, VMEM, ANY],
        out_specs=[VMEM] * 6,
        out_shape=[jax.ShapeDtypeStruct(shape, BF16) for shape in (block, twice, twice, block, block, block)],
        scratch_shapes=[pltpu.VMEM(states.shape, BF16)] * 2 + [pltpu.SemaphoreType.DMA((PATCHES,))],
        compiler_params=SMALL,
        cost_estimate=COST,
        name="apply_weights",
    )(inner, outer, states)


def gather_kernel(c0, c2, c6, c1, c7, c4, c3, c5, out, sems):
    me = lax.axis_index("mem")
    parts = ((c0, 0), (c1, 1), (c2, 2), (c3, 3), (c4, 4), (c5, 5), (c6, 6), (c7, 7))
    copies = []
    for ref, places in parts:
        source = lax.rem(me + PEERS - places, PEERS)
        copies.append(pltpu.make_async_copy(ref.at[pl.ds(0, PATCHES)], out.at[source], sems.at[places]))
    start_all(copies)
    for copy in copies:
        copy.wait()


def gather(*parts):
    shape = (PEERS,) + parts[0].shape
    return pl.pallas_call(
        gather_kernel,
        in_specs=[VMEM] * PEERS,
        out_specs=ANY,
        out_shape=jax.ShapeDtypeStruct(shape, BF16),
        scratch_shapes=[pltpu.SemaphoreType.DMA((PEERS,))],
        compiler_params=SMALL,
        cost_estimate=COST,
        name="gather",
    )(*parts)


def swap(value):
    return lax.all_to_all(value, "mem", split_axis=0, concat_axis=0, tiled=True)


def shift(value, axis, by):
    peers = lax.axis_size(axis)
    return lax.ppermute(value, axis, [(i, (i + by) % peers) for i in range(peers)])


def pair(value, axis, first):
    peers = lax.axis_size(axis)
    pairs = [((i + first) % peers, (i + 1 + first) % peers) for i in range(0, peers, 2)]
    return lax.ppermute(value, axis, pairs + [(j, i) for i, j in pairs])


def spread(c0, c2, c6, c1, c7, c4):
    c2 = shift(c2, "mem", 2)
    c6 = shift(c6, "mem", -2)
    c1 = shift(c1, "mem", 1)
    c7 = shift(c7, "mem", -1)
    c4 = shift(c4, "mem", 4)
    c3 = shift(c2[PATCHES:], "mem", 1)
    c5 = shift(c6[PATCHES:], "mem", -1)
    return gather(c0, c2, c6, c1, c7, c4, c3, c5)


def body(background, obs_ensemble, innovation, obs_precision, taper_weight, obs_count):
    rows = background.shape[3]
    background = background.reshape(PEERS, PATCHES, K // PEERS, rows)
    obs = (obs_count.reshape(PATCHES), obs_ensemble, innovation, obs_precision, taper_weight.transpose(0, 2, 1, 3))
    states = swap(background)
    near, far, following, previous = sent_grams(*obs)
    near = pair(near, "reg", 0)
    far = pair(far, "reg", 1)
    following = shift(following, "mem", 1)
    previous = shift(previous, "mem", -1)
    own = kept_grams(*obs)
    inner = root_weights((1, 2), own, near, far)
    outer = root_weights((0, 3), own, near, far, following, previous)
    analysis = spread(*apply_weights(inner, outer, states))
    return analysis.reshape(1, PEERS * PATCHES, K // PEERS, rows)


def solution(mesh):
    in_specs = (
        P("reg", None, "mem", None),
        P("reg", "mem", None, None),
        P("reg", "mem", None),
        P("reg", "mem", None),
        P("reg", "mem", None, None),
        P("reg", "mem"),
    )
    out_specs = P("reg", None, "mem", None)
    return jax.shard_map(body, mesh=mesh, in_specs=in_specs, out_specs=out_specs, check_vma=False)
```

```python
import functools
import jax
import jax.numpy as jnp
from jax import lax
from jax.experimental import pallas as pl
from jax.experimental.pallas import tpu as pltpu
from jax.sharding import PartitionSpec as P

F32 = jnp.float32
BF16 = jnp.bfloat16
ITERS = 12
ROOT_COST = 2 * 10**9
INNER = (1, 2)
OUTER = (0, 3)
PATCHES = 4
SIDES = 5
K = 256
SLOTS = 2048
PEERS = 8
EXT = K + 8
VMEM = pl.BlockSpec(memory_space=pltpu.VMEM)
SMEM = pl.BlockSpec(memory_space=pltpu.SMEM)
ANY = pl.BlockSpec(memory_space=pl.ANY)
PARAMS = pltpu.CompilerParams(vmem_limit_bytes=24 << 20)
SMALL = pltpu.CompilerParams(vmem_limit_bytes=16 << 20)
COST = pl.CostEstimate(flops=1000, bytes_accessed=1000, transcendentals=0)


def dot(a, b):
    return jnp.dot(a, b, preferred_element_type=F32)


def split(x):
    high = x.astype(BF16)
    return high, (x - high.astype(F32)).astype(BF16)


def start_all(copies):
    for copy in copies:
        copy.start()


def pick_row(value, p):
    patch = lax.broadcasted_iota(jnp.int32, (PATCHES, SLOTS), 0)
    return jnp.sum(jnp.where(patch == p, value.astype(F32), 0.0), axis=0, keepdims=True)


def slot_weights(p, count_ref, prec_ref, taper_ref):
    slot = lax.broadcasted_iota(jnp.int32, (1, SLOTS), 1)
    prec = jnp.where(slot < count_ref[p], pick_row(prec_ref[0], p), 0.0)
    return [prec * pick_row(taper_ref[0, d], p) for d in range(SIDES)]


def weighted_grams(ens_ref, flipped_ref, rows, innov):
    flipped_ref[0:K] = ens_ref[0, 0].T
    flipped_ref[K:] = jnp.broadcast_to(innov, (16, SLOTS)).astype(BF16)
    flipped = flipped_ref[...]
    pairs = []
    for row in rows:
        scaled = (flipped[0:K].astype(F32) * row).astype(BF16)
        both = lax.dot_general(flipped, scaled, (((1,), (1,)), ((), ())), preferred_element_type=F32)
        pairs.append((both[0:K], both[K : K + 1]))
    return pairs


def sent_kernel(count_ref, ens_ref, innov_ref, prec_ref, taper_ref, near_ref, far_ref, next_ref, prev_ref, flipped_ref):
    p = pl.program_id(0)
    even = lax.rem(lax.axis_index("reg"), 2) == 0
    weights = slot_weights(p, count_ref, prec_ref, taper_ref)
    sided = [jnp.where(even, weights[1], weights[2]), jnp.where(even, weights[2], weights[1])]
    innov = pick_row(innov_ref[0], p)

    def store(rows, refs):
        for (gram, drive), ref in zip(weighted_grams(ens_ref, flipped_ref, rows, innov), refs):
            ref[0, 0:K, :] = gram
            ref[0, K:EXT, :] = jnp.broadcast_to(drive, (EXT - K, K))

    @pl.when(p == 0)
    def _():
        store(sided + [weights[4]], (near_ref, far_ref, prev_ref))

    @pl.when((p > 0) & (p < PATCHES - 1))
    def _():
        store(sided, (near_ref, far_ref))

    @pl.when(p == PATCHES - 1)
    def _():
        store(sided + [weights[3]], (near_ref, far_ref, next_ref))


def kept_kernel(count_ref, ens_ref, innov_ref, prec_ref, taper_ref, own_ref, flipped_ref):
    p = pl.program_id(0)
    weights = slot_weights(p, count_ref, prec_ref, taper_ref)
    innov = pick_row(innov_ref[0], p)

    @pl.when(p == 0)
    def _():
        own_ref[...] = jnp.zeros_like(own_ref)

    def add(sides):
        pairs = weighted_grams(ens_ref, flipped_ref, [weights[d] for d in sides], innov)
        for d, (gram, drive) in zip(sides, pairs):
            to = p + {0: 0, 3: 1, 4: -1}[d]
            own_ref[to, 0:K, :] += gram
            own_ref[to, K : K + 1, :] += drive

    @pl.when(p == 0)
    def _():
        add((0, 3))

    @pl.when((p > 0) & (p < PATCHES - 1))
    def _():
        add((0, 3, 4))

    @pl.when(p == PATCHES - 1)
    def _():
        add((0, 4))


def gram_specs():
    return [
        SMEM,
        pl.BlockSpec((1, 1, SLOTS, K), lambda p: (0, p, 0, 0)),
        pl.BlockSpec((1, PATCHES, SLOTS), lambda p: (0, 0, 0)),
        pl.BlockSpec((1, PATCHES, SLOTS), lambda p: (0, 0, 0)),
        pl.BlockSpec((1, SIDES, PATCHES, SLOTS), lambda p: (0, 0, 0, 0)),
    ]


def sent_grams(*args):
    full = jax.ShapeDtypeStruct((PATCHES, EXT, K), F32)
    one = jax.ShapeDtypeStruct((1, EXT, K), F32)
    return pl.pallas_call(
        sent_kernel,
        grid=(PATCHES,),
        in_specs=gram_specs(),
        out_specs=[pl.BlockSpec((1, EXT, K), lambda p: (p, 0, 0))] * 2 + [pl.BlockSpec((1, EXT, K), lambda p: (0, 0, 0))] * 2,
        out_shape=[full, full, one, one],
        scratch_shapes=[pltpu.VMEM((K + 16, SLOTS), BF16)],
        compiler_params=PARAMS,
        cost_estimate=COST,
        name="sent_grams",
    )(*args)


def kept_grams(*args):
    return pl.pallas_call(
        kept_kernel,
        grid=(PATCHES,),
        in_specs=gram_specs(),
        out_specs=pl.BlockSpec((PATCHES, EXT, K), lambda p: (0, 0, 0)),
        out_shape=jax.ShapeDtypeStruct((PATCHES, EXT, K), F32),
        scratch_shapes=[pltpu.VMEM((K + 16, SLOTS), BF16)],
        compiler_params=PARAMS,
        cost_estimate=COST,
        name="kept_grams",
    )(*args)


def split_to(refs, p, x):
    refs[0][p], refs[1][p] = split(x)


def root_kernel(edges, *refs):
    n = 2
    if edges:
        sums, following, previous, out_ref, *rest = refs
        pairs = [[(sums, 0, 0, 0), (following, 0, 1, 0)], [(sums, 1, 0, 1), (previous, 0, 1, 1)]]
    else:
        *parts, out_ref, sums_ref, rest_s, rest_sems = refs[:5] + refs[-2:]
        rest = refs[5:-2]
        pairs = [[(ref, p, w, i) for w, ref in enumerate(parts)] for i, p in enumerate(INNER)]
    held, sems, yh, yl, zh, zl, sh, sl, diag_ref, scale_ref = rest
    y, z, s = (yh, yl), (zh, zl), (sh, sl)
    copies = [
        [pltpu.make_async_copy(ref.at[at], held.at[w, i], sems.at[p, j]) for j, (ref, at, w, i) in enumerate(pairs[p])]
        for p in range(n)
    ]
    for p in range(n):
        start_all(copies[p])
    if not edges:
        others = [
            pltpu.make_async_copy(ref.at[p], rest_s.at[w, i], rest_sems.at[w, i])
            for w, ref in enumerate(parts)
            for i, p in enumerate(OUTER)
        ]
        start_all(others)
    row = lax.broadcasted_iota(jnp.int32, (K, K), 0)
    col = lax.broadcasted_iota(jnp.int32, (K, K), 1)
    diag_ref[...] = jnp.where(row == col, 1.5, 0.0).astype(F32)

    def total(p, part):
        value = held[0, p, part, :]
        for w in range(1, held.shape[0]):
            value = value + held[w, p, part, :]
        return value

    def product(a, b, p):
        ah, al, bh, bl = a[0][p], a[1][p], b[0][p], b[1][p]
        return dot(jnp.concatenate([ah, ah, al], axis=1), jnp.concatenate([bl, bh, bh], axis=0))

    def residual(p):
        split_to(s, p, diag_ref[...] - 0.5 * product(z, y, p))

    for p in range(n):
        for copy in copies[p]:
            copy.wait()
        system = total(p, slice(0, K)) + jnp.where(row == col, float(K - 1), 0.0)
        bound = jnp.max(jnp.sum(jnp.abs(system), axis=0, keepdims=True), axis=1, keepdims=True)
        scale_ref[p] = jnp.broadcast_to(1.0 / jnp.sqrt(bound), (8, K))
        root = system / bound
        split_to(y, p, root)
        split_to(z, p, diag_ref[...] - 0.5 * root)
    for p in range(n):
        split_to(y, p, product(y, z, p))

    def sweep(index, carry):
        for p in range(n):
            residual(p)
        for p in range(n):
            split_to(y, p, product(y, s, p))
            split_to(z, p, product(s, z, p))
        return carry

    lax.fori_loop(0, ITERS - 2, sweep, 0, unroll=True)
    for p in range(n):
        residual(p)
    for p in range(n):
        flipped = product(s, z, p) * scale_ref[p, 0:1, :]
        half = flipped.T
        inner = jnp.sum(half * total(p, slice(K, K + 1)), axis=1, keepdims=True)
        mean_weight = jnp.sum(flipped * inner, axis=0, keepdims=True)
        out_ref[p] = (jnp.sqrt(float(K - 1)) * flipped + mean_weight).astype(BF16)
    if not edges:
        for copy in others:
            copy.wait()
        for i in range(n):
            sums_ref[i] = rest_s[0, i] + rest_s[1, i] + rest_s[2, i]


def root_weights(edges, *args):
    n = 2
    piece = pltpu.VMEM((n, K, K), BF16)
    parts = 2 if edges else 3
    held, sems = pltpu.VMEM((parts, n, EXT, K), F32), pltpu.SemaphoreType.DMA((parts, max(n, parts)))
    shapes = [jax.ShapeDtypeStruct((n, K, K), BF16)] + ([] if edges else [jax.ShapeDtypeStruct((n, EXT, K), F32)])
    return pl.pallas_call(
        functools.partial(root_kernel, edges),
        in_specs=[ANY] * len(args),
        out_specs=[VMEM] * len(shapes),
        out_shape=shapes,
        scratch_shapes=[held, sems]
        + [piece] * 6
        + [pltpu.VMEM((K, K), F32), pltpu.VMEM((n, 8, K), F32)]
        + ([] if edges else [held, sems]),
        compiler_params=PARAMS,
        cost_estimate=pl.CostEstimate(flops=ROOT_COST, bytes_accessed=1000, transcendentals=0),
        name="root_weights",
    )(*args)


def analysed(states, flipped):
    states = states.astype(F32)
    mean = jnp.sum(states, axis=0, keepdims=True) * (1.0 / K)
    return (mean + dot(flipped, (states - mean).astype(BF16))).astype(BF16)


def apply_kernel(patches, flipped_ref, states, *refs):
    *out_refs, states_s, sems = refs
    rows = states_s.shape[3]
    copies = [pltpu.make_async_copy(states.at[:, p], states_s.at[:, i], sems.at[i]) for i, p in enumerate(patches)]
    start_all(copies)
    whole = out_refs[-1]
    for i in range(len(patches)):
        copies[i].wait()
        whole[:, i] = analysed(states_s[:, i].reshape(K, rows), flipped_ref[i]).reshape(PEERS, K // PEERS, rows)
    if len(out_refs) == 1:
        return
    c0, c2, c6, c1, c7, c4 = out_refs[:6]
    me = lax.axis_index("mem")

    def away(places):
        return whole[lax.rem(me + places, PEERS)]

    n = len(patches)
    c0[...] = away(0)
    c2[0:n] = away(2)
    c2[n:] = away(3)
    c6[0:n] = away(6)
    c6[n:] = away(5)
    c1[...] = away(1)
    c7[...] = away(7)
    c4[...] = away(4)


def apply_weights(patches, flipped, states, turned):
    n = len(patches)
    block = (n,) + states.shape[2:]
    twice = (2 * n,) + states.shape[2:]
    whole = pltpu.VMEM((PEERS,) + block, BF16)
    shapes = (block, twice, twice, block, block, block) if turned else ((PEERS,) + block,)
    return pl.pallas_call(
        functools.partial(apply_kernel, patches),
        in_specs=[VMEM, ANY],
        out_specs=[VMEM] * len(shapes),
        out_shape=[jax.ShapeDtypeStruct(shape, BF16) for shape in shapes],
        scratch_shapes=[whole] * (2 if turned else 1) + [pltpu.SemaphoreType.DMA((n,))],
        compiler_params=SMALL,
        cost_estimate=COST,
        name="apply_weights",
    )(flipped, states)


def gather_kernel(first, c0, c2, c6, c1, c7, c4, c3, c5, out, sems):
    me = lax.axis_index("mem")
    parts = ((c0, 0), (c1, 1), (c2, 2), (c3, 3), (c4, 4), (c5, 5), (c6, 6), (c7, 7))
    copies = []
    for j in range(PEERS):
        copies.append(pltpu.make_async_copy(first.at[j], out.at[j, pl.ds(1, 2)], sems.at[j]))
    for ref, places in parts:
        source = lax.rem(me + PEERS - places, PEERS)
        for i, p in enumerate(OUTER):
            copies.append(pltpu.make_async_copy(ref.at[i], out.at[source, p], sems.at[PEERS + 2 * places + i]))
    start_all(copies)
    for copy in copies:
        copy.wait()


def gather(first, *parts):
    shape = (PEERS, PATCHES) + first.shape[2:]
    return pl.pallas_call(
        gather_kernel,
        in_specs=[VMEM] * (PEERS + 1),
        out_specs=ANY,
        out_shape=jax.ShapeDtypeStruct(shape, BF16),
        scratch_shapes=[pltpu.SemaphoreType.DMA((3 * PEERS,))],
        compiler_params=SMALL,
        cost_estimate=COST,
        name="gather",
    )(first, *parts)


def swap(value):
    return lax.all_to_all(value, "mem", split_axis=0, concat_axis=0, tiled=True)


def shift(value, axis, by):
    peers = lax.axis_size(axis)
    return lax.ppermute(value, axis, [(i, (i + by) % peers) for i in range(peers)])


def pair(value, axis, first):
    peers = lax.axis_size(axis)
    pairs = [((i + first) % peers, (i + 1 + first) % peers) for i in range(0, peers, 2)]
    return lax.ppermute(value, axis, pairs + [(j, i) for i, j in pairs])


def spread(c0, c2, c6, c1, c7, c4):
    n = c0.shape[0]
    c2 = shift(c2, "mem", 2)
    c6 = shift(c6, "mem", -2)
    c1 = shift(c1, "mem", 1)
    c7 = shift(c7, "mem", -1)
    c4 = shift(c4, "mem", 4)
    c3 = shift(c2[n:], "mem", 1)
    c5 = shift(c6[n:], "mem", -1)
    return c0, c2, c6, c1, c7, c4, c3, c5


def body(background, obs_ensemble, innovation, obs_precision, taper_weight, obs_count):
    rows = background.shape[3]
    background = background.reshape(PEERS, PATCHES, K // PEERS, rows)
    obs = (obs_count.reshape(PATCHES), obs_ensemble, innovation, obs_precision, taper_weight.transpose(0, 2, 1, 3))
    states = swap(background)
    near, far, following, previous = sent_grams(*obs)
    near = pair(near, "reg", 0)
    far = pair(far, "reg", 1)
    following = shift(following, "mem", 1)
    previous = shift(previous, "mem", -1)
    own = kept_grams(*obs)
    flipped, sums = root_weights(False, own, near, far)
    (first,) = apply_weights(INNER, flipped, states, False)
    first, following, previous = lax.optimization_barrier((first, following, previous))
    first = swap(first)
    (flipped,) = root_weights(True, sums, following, previous)
    analysis = gather(first, *spread(*apply_weights(OUTER, flipped, states, True)))
    return analysis.reshape(1, PEERS * PATCHES, K // PEERS, rows)


def solution(mesh):
    in_specs = (
        P("reg", None, "mem", None),
        P("reg", "mem", None, None),
        P("reg", "mem", None),
        P("reg", "mem", None),
        P("reg", "mem", None, None),
        P("reg", "mem"),
    )
    out_specs = P("reg", None, "mem", None)
    return jax.shard_map(body, mesh=mesh, in_specs=in_specs, out_specs=out_specs, check_vma=False)
```

```python
import functools
import jax
import jax.numpy as jnp
from jax import lax
from jax.experimental import pallas as pl
from jax.experimental.pallas import tpu as pltpu
from jax.sharding import PartitionSpec as P

F32 = jnp.float32
BF16 = jnp.bfloat16
ITERS = 12
ROOT_COST = 2 * 10**9
INNER = (1, 2)
OUTER = (0, 3)
PATCHES = 4
SIDES = 5
K = 256
SLOTS = 2048
PEERS = 8
EXT = K + 8
HALF = K // 2
EDGE = HALF + 8
VMEM = pl.BlockSpec(memory_space=pltpu.VMEM)
SMEM = pl.BlockSpec(memory_space=pltpu.SMEM)
ANY = pl.BlockSpec(memory_space=pl.ANY)
PARAMS = pltpu.CompilerParams(vmem_limit_bytes=24 << 20)
SMALL = pltpu.CompilerParams(vmem_limit_bytes=16 << 20)
COST = pl.CostEstimate(flops=1000, bytes_accessed=1000, transcendentals=0)


def dot(a, b):
    return jnp.dot(a, b, preferred_element_type=F32)


def split(x):
    high = x.astype(BF16)
    return high, (x - high.astype(F32)).astype(BF16)


def start_all(copies):
    for copy in copies:
        copy.start()


def pick_row(value, p):
    patch = lax.broadcasted_iota(jnp.int32, (PATCHES, SLOTS), 0)
    return jnp.sum(jnp.where(patch == p, value.astype(F32), 0.0), axis=0, keepdims=True)


def slot_weights(p, count_ref, prec_ref, taper_ref):
    slot = lax.broadcasted_iota(jnp.int32, (1, SLOTS), 1)
    prec = jnp.where(slot < count_ref[p], pick_row(prec_ref[0], p), 0.0)
    return [prec * pick_row(taper_ref[0, d], p) for d in range(SIDES)]


def weighted_grams(ens_ref, flipped_ref, rows, innov):
    flipped_ref[0:K] = ens_ref[0, 0].T
    flipped_ref[K:] = jnp.broadcast_to(innov, (16, SLOTS)).astype(BF16)
    flipped = flipped_ref[...]
    pairs = []
    for row in rows:
        scaled = (flipped[0:K].astype(F32) * row).astype(BF16)
        both = lax.dot_general(flipped, scaled, (((1,), (1,)), ((), ())), preferred_element_type=F32)
        pairs.append((both[0:K], both[K : K + 1]))
    return pairs


def upper_lower(n):
    row = lax.broadcasted_iota(jnp.int32, (n, n), 0)
    col = lax.broadcasted_iota(jnp.int32, (n, n), 1)
    return row <= col, row == col


def diagonal(gram):
    return jnp.sum(jnp.where(upper_lower(K)[1], gram, 0.0), axis=0, keepdims=True)


def unpacked(packed, diag):
    upper, same = upper_lower(packed.shape[0])
    flipped = packed.T
    return jnp.where(upper, packed, flipped), jnp.where(same, diag, jnp.where(upper, flipped, packed))


def unfolded(ref):
    ahead, behind = unpacked(ref[0:HALF, 0:HALF], ref[HALF + 1 : HALF + 2, HALF:])
    across = ref[0:HALF, HALF:]
    return jnp.concatenate(
        [jnp.concatenate([ahead, across], axis=1), jnp.concatenate([across.T, behind], axis=1)], axis=0
    )


def sent_kernel(count_ref, ens_ref, innov_ref, prec_ref, taper_ref, near_ref, far_ref, next_ref, prev_ref, flipped_ref):
    even = lax.rem(lax.axis_index("reg"), 2) == 0
    for p in range(PATCHES):

        @pl.when(pl.program_id(0) == p)
        def _():
            weights = slot_weights(p, count_ref, prec_ref, taper_ref)
            rows = [jnp.where(even, weights[1], weights[2]), jnp.where(even, weights[2], weights[1])]
            rows += {0: [weights[4]], PATCHES - 1: [weights[3]]}.get(p, [])
            (near, near_drive), (far, far_drive), *edge = weighted_grams(ens_ref, flipped_ref, rows, pick_row(innov_ref[0], p))
            near_ref[0, 0:K, :] = near
            near_ref[0, K:EXT, :] = jnp.broadcast_to(near_drive, (EXT - K, K))
            if p < 2:
                far_ref[p, 0:K, :] = far
                far_ref[p, K:EXT, :] = jnp.broadcast_to(far_drive, (EXT - K, K))
            else:
                at = PATCHES - 1 - p
                far_ref[at, 0:K, :] = jnp.where(upper_lower(K)[0], far_ref[at, 0:K, :], far)
                far_ref[at, K + 1 : K + 2, :] = far_drive
                far_ref[at, K + 2 : K + 3, :] = diagonal(far)
            for (gram, drive), ref in zip(edge, (next_ref if p else prev_ref,)):
                ref[0, 0:HALF, 0:HALF] = jnp.where(upper_lower(HALF)[0], gram[0:HALF, 0:HALF], gram[HALF:, HALF:])
                ref[0, 0:HALF, HALF:] = gram[0:HALF, HALF:]
                ref[0, HALF:, :] = jnp.broadcast_to(drive, (EDGE - HALF, K))
                ref[0, HALF + 1 : HALF + 2, :] = diagonal(gram)


def kept_kernel(count_ref, ens_ref, innov_ref, prec_ref, taper_ref, own_ref, flipped_ref):
    p = pl.program_id(0)
    weights = slot_weights(p, count_ref, prec_ref, taper_ref)
    innov = pick_row(innov_ref[0], p)

    @pl.when(p == 0)
    def _():
        own_ref[...] = jnp.zeros_like(own_ref)

    def add(sides):
        pairs = weighted_grams(ens_ref, flipped_ref, [weights[d] for d in sides], innov)
        for d, (gram, drive) in zip(sides, pairs):
            to = p + {0: 0, 3: 1, 4: -1}[d]
            own_ref[to, 0:K, :] += gram
            own_ref[to, K : K + 1, :] += drive

    @pl.when(p == 0)
    def _():
        add((0, 3))

    @pl.when((p > 0) & (p < PATCHES - 1))
    def _():
        add((0, 3, 4))

    @pl.when(p == PATCHES - 1)
    def _():
        add((0, 4))


def gram_specs():
    return [
        SMEM,
        pl.BlockSpec((1, 1, SLOTS, K), lambda p: (0, p, 0, 0)),
        pl.BlockSpec((1, PATCHES, SLOTS), lambda p: (0, 0, 0)),
        pl.BlockSpec((1, PATCHES, SLOTS), lambda p: (0, 0, 0)),
        pl.BlockSpec((1, SIDES, PATCHES, SLOTS), lambda p: (0, 0, 0, 0)),
    ]


def sent_grams(*args):
    full = jax.ShapeDtypeStruct((PATCHES, EXT, K), F32)
    two = jax.ShapeDtypeStruct((2, EXT, K), F32)
    one = jax.ShapeDtypeStruct((1, EDGE, K), F32)
    return pl.pallas_call(
        sent_kernel,
        grid=(PATCHES,),
        in_specs=gram_specs(),
        out_specs=[pl.BlockSpec((1, EXT, K), lambda p: (p, 0, 0)), pl.BlockSpec((2, EXT, K), lambda p: (0, 0, 0))]
        + [pl.BlockSpec((1, EDGE, K), lambda p: (0, 0, 0))] * 2,
        out_shape=[full, two, one, one],
        scratch_shapes=[pltpu.VMEM((K + 16, SLOTS), BF16)],
        compiler_params=PARAMS,
        cost_estimate=COST,
        name="sent_grams",
    )(*args)


def kept_grams(*args):
    return pl.pallas_call(
        kept_kernel,
        grid=(PATCHES,),
        in_specs=gram_specs(),
        out_specs=pl.BlockSpec((PATCHES, EXT, K), lambda p: (0, 0, 0)),
        out_shape=jax.ShapeDtypeStruct((PATCHES, EXT, K), F32),
        scratch_shapes=[pltpu.VMEM((K + 16, SLOTS), BF16)],
        compiler_params=PARAMS,
        cost_estimate=COST,
        name="kept_grams",
    )(*args)


def split_to(refs, p, x):
    refs[0][p], refs[1][p] = split(x)


def root_kernel(edges, *refs):
    n = 2
    if edges:
        sums, following, previous, out_ref, total_s, edge_s, *rest = refs
        sources = [(sums, total_s), (following, edge_s.at[pl.ds(0, 1)]), (previous, edge_s.at[pl.ds(1, 1)])]
    else:
        own, near, far, out_ref, sums_ref, total_s, own_s, near_s, far_s, *rest = refs
        sources = [(own, own_s), (near, near_s), (far, far_s)]
    sems, yh, yl, zh, zl, sh, sl, diag_ref, scale_ref = rest
    y, z, s = (yh, yl), (zh, zl), (sh, sl)
    copies = [pltpu.make_async_copy(a, b, sems.at[i]) for i, (a, b) in enumerate(sources)]
    start_all(copies)
    row = lax.broadcasted_iota(jnp.int32, (K, K), 0)
    col = lax.broadcasted_iota(jnp.int32, (K, K), 1)
    diag_ref[...] = jnp.where(row == col, 1.5, 0.0).astype(F32)

    def add_up(ref, patches, pair):
        packed = far_s[pair, 0:K, :]
        for i, (p, gram) in enumerate(zip(patches, unpacked(packed, far_s[pair, K + 2 : K + 3, :]))):
            ref[i, 0:K, :] = own_s[p, 0:K, :] + near_s[p, 0:K, :] + gram
            ref[i, K : K + 1, :] = own_s[p, K : K + 1, :] + near_s[p, K : K + 1, :] + far_s[pair, K + i : K + i + 1, :]

    def product(a, b, p):
        ah, al, bh, bl = a[0][p], a[1][p], b[0][p], b[1][p]
        return dot(jnp.concatenate([ah, ah, al], axis=1), jnp.concatenate([bl, bh, bh], axis=0))

    def residual(p):
        split_to(s, p, diag_ref[...] - 0.5 * product(z, y, p))

    for copy in copies:
        copy.wait()
    if not edges:
        add_up(total_s, INNER, 1)
    for p in range(n):
        if edges:
            total_s[p, 0:K, :] += unfolded(edge_s.at[p])
            total_s[p, K : K + 1, :] += edge_s[p, HALF : HALF + 1, :]
        system = total_s[p, 0:K, :] + jnp.where(row == col, float(K - 1), 0.0)
        bound = jnp.max(jnp.sum(jnp.abs(system), axis=0, keepdims=True), axis=1, keepdims=True)
        scale_ref[p] = jnp.broadcast_to(1.0 / jnp.sqrt(bound), (8, K))
        root = system / bound
        split_to(y, p, root)
        split_to(z, p, diag_ref[...] - 0.5 * root)
    for p in range(n):
        split_to(y, p, product(y, z, p))

    def sweep(index, carry):
        for p in range(n):
            residual(p)
        for p in range(n):
            split_to(y, p, product(y, s, p))
            split_to(z, p, product(s, z, p))
        return carry

    lax.fori_loop(0, ITERS - 2, sweep, 0, unroll=True)
    for p in range(n):
        residual(p)
    for p in range(n):
        flipped = product(s, z, p) * scale_ref[p, 0:1, :]
        half = flipped.T
        inner = jnp.sum(half * total_s[p, K : K + 1, :], axis=1, keepdims=True)
        mean_weight = jnp.sum(flipped * inner, axis=0, keepdims=True)
        out_ref[p] = (jnp.sqrt(float(K - 1)) * flipped + mean_weight).astype(BF16)
    if not edges:
        add_up(sums_ref, OUTER, 0)


def root_weights(edges, *args):
    n = 2
    piece = pltpu.VMEM((n, K, K), BF16)
    two, full, edge = (pltpu.VMEM(shape, F32) for shape in ((n, EXT, K), (PATCHES, EXT, K), (2, EDGE, K)))
    shapes = [jax.ShapeDtypeStruct((n, K, K), BF16)] + ([] if edges else [jax.ShapeDtypeStruct((n, EXT, K), F32)])
    return pl.pallas_call(
        functools.partial(root_kernel, edges),
        in_specs=[ANY] * len(args),
        out_specs=[VMEM] * len(shapes),
        out_shape=shapes,
        scratch_shapes=([two, edge] if edges else [two, full, full, two])
        + [pltpu.SemaphoreType.DMA((3,))]
        + [piece] * 6
        + [pltpu.VMEM((K, K), F32), pltpu.VMEM((n, 8, K), F32)],
        compiler_params=PARAMS,
        cost_estimate=pl.CostEstimate(flops=ROOT_COST, bytes_accessed=1000, transcendentals=0),
        name="root_weights",
    )(*args)


def analysed(states, flipped):
    states = states.astype(F32)
    mean = jnp.sum(states, axis=0, keepdims=True) * (1.0 / K)
    return (mean + dot(flipped, (states - mean).astype(BF16))).astype(BF16)


def apply_kernel(patches, flipped_ref, states, *refs):
    *out_refs, states_s, sems = refs
    rows = states_s.shape[3]
    copies = [pltpu.make_async_copy(states.at[:, p], states_s.at[:, i], sems.at[i]) for i, p in enumerate(patches)]
    start_all(copies)
    whole = out_refs[-1]
    for i in range(len(patches)):
        copies[i].wait()
        whole[:, i] = analysed(states_s[:, i].reshape(K, rows), flipped_ref[i]).reshape(PEERS, K // PEERS, rows)
    if len(out_refs) == 1:
        return
    c0, c2, c6, c1, c7, c4 = out_refs[:6]
    me = lax.axis_index("mem")

    def away(places):
        return whole[lax.rem(me + places, PEERS)]

    n = len(patches)
    c0[...] = away(0)
    c2[0:n] = away(2)
    c2[n:] = away(3)
    c6[0:n] = away(6)
    c6[n:] = away(5)
    c1[...] = away(1)
    c7[...] = away(7)
    c4[...] = away(4)


def apply_weights(patches, flipped, states, turned):
    n = len(patches)
    block = (n,) + states.shape[2:]
    twice = (2 * n,) + states.shape[2:]
    whole = pltpu.VMEM((PEERS,) + block, BF16)
    shapes = (block, twice, twice, block, block, block) if turned else ((PEERS,) + block,)
    return pl.pallas_call(
        functools.partial(apply_kernel, patches),
        in_specs=[VMEM, ANY],
        out_specs=[VMEM] * len(shapes),
        out_shape=[jax.ShapeDtypeStruct(shape, BF16) for shape in shapes],
        scratch_shapes=[whole] * (2 if turned else 1) + [pltpu.SemaphoreType.DMA((n,))],
        compiler_params=SMALL,
        cost_estimate=COST,
        name="apply_weights",
    )(flipped, states)


def gather_kernel(first, c0, c2, c6, c1, c7, c4, c3, c5, out, sems):
    me = lax.axis_index("mem")
    parts = ((c0, 0), (c1, 1), (c2, 2), (c3, 3), (c4, 4), (c5, 5), (c6, 6), (c7, 7))
    copies = []
    for j in range(PEERS):
        copies.append(pltpu.make_async_copy(first.at[j], out.at[j, pl.ds(1, 2)], sems.at[j]))
    for ref, places in parts:
        source = lax.rem(me + PEERS - places, PEERS)
        for i, p in enumerate(OUTER):
            copies.append(pltpu.make_async_copy(ref.at[i], out.at[source, p], sems.at[PEERS + 2 * places + i]))
    start_all(copies)
    for copy in copies:
        copy.wait()


def gather(first, *parts):
    shape = (PEERS, PATCHES) + first.shape[2:]
    return pl.pallas_call(
        gather_kernel,
        in_specs=[VMEM] * (PEERS + 1),
        out_specs=ANY,
        out_shape=jax.ShapeDtypeStruct(shape, BF16),
        scratch_shapes=[pltpu.SemaphoreType.DMA((3 * PEERS,))],
        compiler_params=SMALL,
        cost_estimate=COST,
        name="gather",
    )(first, *parts)


def swap(value):
    return lax.all_to_all(value, "mem", split_axis=0, concat_axis=0, tiled=True)


def shift(value, axis, by):
    peers = lax.axis_size(axis)
    return lax.ppermute(value, axis, [(i, (i + by) % peers) for i in range(peers)])


def pair(value, axis, first):
    peers = lax.axis_size(axis)
    pairs = [((i + first) % peers, (i + 1 + first) % peers) for i in range(0, peers, 2)]
    return lax.ppermute(value, axis, pairs + [(j, i) for i, j in pairs])


def spread(c0, c2, c6, c1, c7, c4):
    n = c0.shape[0]
    c2 = shift(c2, "mem", 2)
    c6 = shift(c6, "mem", -2)
    c1 = shift(c1, "mem", 1)
    c7 = shift(c7, "mem", -1)
    c4 = shift(c4, "mem", 4)
    c3 = shift(c2[n:], "mem", 1)
    c5 = shift(c6[n:], "mem", -1)
    return c0, c2, c6, c1, c7, c4, c3, c5


def body(background, obs_ensemble, innovation, obs_precision, taper_weight, obs_count):
    rows = background.shape[3]
    background = background.reshape(PEERS, PATCHES, K // PEERS, rows)
    obs = (obs_count.reshape(PATCHES), obs_ensemble, innovation, obs_precision, taper_weight.transpose(0, 2, 1, 3))
    states = swap(background)
    near, far, following, previous = sent_grams(*obs)
    near = pair(near, "reg", 0)
    far = pair(far, "reg", 1)
    following = shift(following, "mem", 1)
    previous = shift(previous, "mem", -1)
    own = kept_grams(*obs)
    flipped, sums = root_weights(False, own, near, far)
    (first,) = apply_weights(INNER, flipped, states, False)
    first, following, previous = lax.optimization_barrier((first, following, previous))
    first = swap(first)
    (flipped,) = root_weights(True, sums, following, previous)
    analysis = gather(first, *spread(*apply_weights(OUTER, flipped, states, True)))
    return analysis.reshape(1, PEERS * PATCHES, K // PEERS, rows)


def solution(mesh):
    in_specs = (
        P("reg", None, "mem", None),
        P("reg", "mem", None, None),
        P("reg", "mem", None),
        P("reg", "mem", None),
        P("reg", "mem", None, None),
        P("reg", "mem"),
    )
    out_specs = P("reg", None, "mem", None)
    return jax.shard_map(body, mesh=mesh, in_specs=in_specs, out_specs=out_specs, check_vma=False)
```

```python
import functools
import jax
import jax.numpy as jnp
from jax import lax
from jax.experimental import pallas as pl
from jax.experimental.pallas import tpu as pltpu
from jax.sharding import PartitionSpec as P

F32 = jnp.float32
BF16 = jnp.bfloat16
ITERS = 12
ROOT_COST = 2 * 10**9
INNER = (1, 2)
OUTER = (0, 3)
PATCHES = 4
SIDES = 5
K = 256
SLOTS = 2048
PEERS = 8
EXT = K + 8
HALF = K // 2
EDGE = HALF + 8
VMEM = pl.BlockSpec(memory_space=pltpu.VMEM)
SMEM = pl.BlockSpec(memory_space=pltpu.SMEM)
ANY = pl.BlockSpec(memory_space=pl.ANY)
PARAMS = pltpu.CompilerParams(vmem_limit_bytes=24 << 20)
SMALL = pltpu.CompilerParams(vmem_limit_bytes=16 << 20)
COST = pl.CostEstimate(flops=1000, bytes_accessed=1000, transcendentals=0)


def dot(a, b):
    return jnp.dot(a, b, preferred_element_type=F32)


def split(x):
    high = x.astype(BF16)
    return high, (x - high.astype(F32)).astype(BF16)


def start_all(copies):
    for copy in copies:
        copy.start()


def pick_row(value, p):
    patch = lax.broadcasted_iota(jnp.int32, (PATCHES, SLOTS), 0)
    return jnp.sum(jnp.where(patch == p, value.astype(F32), 0.0), axis=0, keepdims=True)


def slot_weights(p, count_ref, prec_ref, taper_ref):
    slot = lax.broadcasted_iota(jnp.int32, (1, SLOTS), 1)
    prec = jnp.where(slot < count_ref[p], pick_row(prec_ref[0], p), 0.0)
    return [prec * pick_row(taper_ref[0, d], p) for d in range(SIDES)]


def weighted_grams(ens_ref, flipped_ref, rows, innov):
    flipped_ref[0:K] = ens_ref[0, 0].T
    flipped_ref[K:] = jnp.broadcast_to(innov, (16, SLOTS)).astype(BF16)
    flipped = flipped_ref[...]
    pairs = []
    for row in rows:
        scaled = (flipped[0:K].astype(F32) * row).astype(BF16)
        both = lax.dot_general(flipped, scaled, (((1,), (1,)), ((), ())), preferred_element_type=F32)
        pairs.append((both[0:K], both[K : K + 1]))
    return pairs


def upper_lower(n):
    row = lax.broadcasted_iota(jnp.int32, (n, n), 0)
    col = lax.broadcasted_iota(jnp.int32, (n, n), 1)
    return row <= col, row == col


def diagonal(gram):
    return jnp.sum(jnp.where(upper_lower(K)[1], gram, 0.0), axis=0, keepdims=True)


def unpacked(packed, diag):
    upper, same = upper_lower(packed.shape[0])
    flipped = packed.T
    return jnp.where(upper, packed, flipped), jnp.where(same, diag, jnp.where(upper, flipped, packed))


def unfolded(ref):
    ahead, behind = unpacked(ref[0:HALF, 0:HALF], ref[HALF + 1 : HALF + 2, HALF:])
    across = ref[0:HALF, HALF:]
    return jnp.concatenate(
        [jnp.concatenate([ahead, across], axis=1), jnp.concatenate([across.T, behind], axis=1)], axis=0
    )


def sent_kernel(count_ref, ens_ref, innov_ref, prec_ref, taper_ref, near_ref, far_ref, next_ref, prev_ref, flipped_ref):
    even = lax.rem(lax.axis_index("reg"), 2) == 0
    for p in range(PATCHES):

        @pl.when(pl.program_id(0) == p)
        def _():
            weights = slot_weights(p, count_ref, prec_ref, taper_ref)
            rows = [jnp.where(even, weights[1], weights[2]), jnp.where(even, weights[2], weights[1])]
            rows += {0: [weights[4]], PATCHES - 1: [weights[3]]}.get(p, [])
            (near, near_drive), (far, far_drive), *edge = weighted_grams(ens_ref, flipped_ref, rows, pick_row(innov_ref[0], p))
            far = 0.5 * (far + far.T)
            near_ref[0, 0:K, :] = near
            near_ref[0, K:EXT, :] = jnp.broadcast_to(near_drive, (EXT - K, K))
            if p < 2:
                far_ref[p, 0:K, :] = far
                far_ref[p, K:EXT, :] = jnp.broadcast_to(far_drive, (EXT - K, K))
            else:
                at = PATCHES - 1 - p
                far_ref[at, 0:K, :] = jnp.where(upper_lower(K)[0], far_ref[at, 0:K, :], far)
                far_ref[at, K + 1 : K + 2, :] = far_drive
                far_ref[at, K + 2 : K + 3, :] = diagonal(far)
            for (gram, drive), ref in zip(edge, (next_ref if p else prev_ref,)):
                gram = 0.5 * (gram + gram.T)
                ref[0, 0:HALF, 0:HALF] = jnp.where(upper_lower(HALF)[0], gram[0:HALF, 0:HALF], gram[HALF:, HALF:])
                ref[0, 0:HALF, HALF:] = gram[0:HALF, HALF:]
                ref[0, HALF:, :] = jnp.broadcast_to(drive, (EDGE - HALF, K))
                ref[0, HALF + 1 : HALF + 2, :] = diagonal(gram)


def kept_kernel(count_ref, ens_ref, innov_ref, prec_ref, taper_ref, own_ref, flipped_ref):
    p = pl.program_id(0)
    weights = slot_weights(p, count_ref, prec_ref, taper_ref)
    innov = pick_row(innov_ref[0], p)

    @pl.when(p == 0)
    def _():
        own_ref[...] = jnp.zeros_like(own_ref)

    def add(sides):
        pairs = weighted_grams(ens_ref, flipped_ref, [weights[d] for d in sides], innov)
        for d, (gram, drive) in zip(sides, pairs):
            to = p + {0: 0, 3: 1, 4: -1}[d]
            own_ref[to, 0:K, :] += gram
            own_ref[to, K : K + 1, :] += drive

    @pl.when(p == 0)
    def _():
        add((0, 3))

    @pl.when((p > 0) & (p < PATCHES - 1))
    def _():
        add((0, 3, 4))

    @pl.when(p == PATCHES - 1)
    def _():
        add((0, 4))


def gram_specs():
    return [
        SMEM,
        pl.BlockSpec((1, 1, SLOTS, K), lambda p: (0, p, 0, 0)),
        pl.BlockSpec((1, PATCHES, SLOTS), lambda p: (0, 0, 0)),
        pl.BlockSpec((1, PATCHES, SLOTS), lambda p: (0, 0, 0)),
        pl.BlockSpec((1, SIDES, PATCHES, SLOTS), lambda p: (0, 0, 0, 0)),
    ]


def sent_grams(*args):
    full = jax.ShapeDtypeStruct((PATCHES, EXT, K), F32)
    two = jax.ShapeDtypeStruct((2, EXT, K), F32)
    one = jax.ShapeDtypeStruct((1, EDGE, K), F32)
    return pl.pallas_call(
        sent_kernel,
        grid=(PATCHES,),
        in_specs=gram_specs(),
        out_specs=[pl.BlockSpec((1, EXT, K), lambda p: (p, 0, 0)), pl.BlockSpec((2, EXT, K), lambda p: (0, 0, 0))]
        + [pl.BlockSpec((1, EDGE, K), lambda p: (0, 0, 0))] * 2,
        out_shape=[full, two, one, one],
        scratch_shapes=[pltpu.VMEM((K + 16, SLOTS), BF16)],
        compiler_params=PARAMS,
        cost_estimate=COST,
        name="sent_grams",
    )(*args)


def kept_grams(*args):
    return pl.pallas_call(
        kept_kernel,
        grid=(PATCHES,),
        in_specs=gram_specs(),
        out_specs=pl.BlockSpec((PATCHES, EXT, K), lambda p: (0, 0, 0)),
        out_shape=jax.ShapeDtypeStruct((PATCHES, EXT, K), F32),
        scratch_shapes=[pltpu.VMEM((K + 16, SLOTS), BF16)],
        compiler_params=PARAMS,
        cost_estimate=COST,
        name="kept_grams",
    )(*args)


def split_to(refs, p, x):
    refs[0][p], refs[1][p] = split(x)


def analysed(states, flipped):
    states = states.astype(F32)
    mean = jnp.sum(states, axis=0, keepdims=True) * (1.0 / K)
    return (mean + dot(flipped, (states - mean).astype(BF16))).astype(BF16)


def cut_for_peers(whole, refs):
    me = lax.axis_index("mem")
    n = whole.shape[1]
    for ref, places in zip(refs, ((0,), (2, 3), (6, 5), (1,), (7,), (4,))):
        for i, away in enumerate(places):
            ref[i * n : (i + 1) * n] = whole[lax.rem(me + away, PEERS)]


def root_kernel(edges, *refs):
    n = 2
    if edges:
        sums, following, previous, states, *refs = refs
        out_refs, (whole, states_s, state_sem, total_s, edge_s, *rest) = refs[:6], refs[6:]
        fetch = pltpu.make_async_copy(states, states_s, state_sem.at[0])
        sources = [(sums, total_s), (following, edge_s.at[pl.ds(0, 1)]), (previous, edge_s.at[pl.ds(1, 1)])]
    else:
        own, near, far, out_ref, sums_ref, total_s, own_s, near_s, far_s, *rest = refs
        sources = [(own, own_s), (near, near_s), (far, far_s)]
    sems, yh, yl, zh, zl, sh, sl, diag_ref, scale_ref = rest
    y, z, s = (yh, yl), (zh, zl), (sh, sl)
    copies = [pltpu.make_async_copy(a, b, sems.at[i]) for i, (a, b) in enumerate(sources)]
    start_all(copies)
    if edges:
        fetch.start()
    row = lax.broadcasted_iota(jnp.int32, (K, K), 0)
    col = lax.broadcasted_iota(jnp.int32, (K, K), 1)
    diag_ref[...] = jnp.where(row == col, 1.5, 0.0).astype(F32)

    def add_up(ref, patches, pair):
        packed = far_s[pair, 0:K, :]
        for i, (p, gram) in enumerate(zip(patches, unpacked(packed, far_s[pair, K + 2 : K + 3, :]))):
            ref[i, 0:K, :] = own_s[p, 0:K, :] + near_s[p, 0:K, :] + gram
            ref[i, K : K + 1, :] = own_s[p, K : K + 1, :] + near_s[p, K : K + 1, :] + far_s[pair, K + i : K + i + 1, :]

    def product(a, b, p):
        ah, al, bh, bl = a[0][p], a[1][p], b[0][p], b[1][p]
        return dot(jnp.concatenate([ah, ah, al], axis=1), jnp.concatenate([bl, bh, bh], axis=0))

    def residual(p):
        split_to(s, p, diag_ref[...] - 0.5 * product(z, y, p))

    for copy in copies:
        copy.wait()
    if not edges:
        add_up(total_s, INNER, 1)
    for p in range(n):
        if edges:
            total_s[p, 0:K, :] += unfolded(edge_s.at[p])
            total_s[p, K : K + 1, :] += edge_s[p, HALF : HALF + 1, :]
        system = total_s[p, 0:K, :] + jnp.where(row == col, float(K - 1), 0.0)
        bound = jnp.max(jnp.sum(jnp.abs(system), axis=0, keepdims=True), axis=1, keepdims=True)
        scale_ref[p] = jnp.broadcast_to(1.0 / jnp.sqrt(bound), (8, K))
        root = system / bound
        split_to(y, p, root)
        split_to(z, p, diag_ref[...] - 0.5 * root)
    for p in range(n):
        split_to(y, p, product(y, z, p))

    def sweep(index, carry):
        for p in range(n):
            residual(p)
        for p in range(n):
            split_to(y, p, product(y, s, p))
            split_to(z, p, product(s, z, p))
        return carry

    lax.fori_loop(0, ITERS - 2, sweep, 0, unroll=True)
    for p in range(n):
        residual(p)
    if edges:
        fetch.wait()
    for p in range(n):
        flipped = product(s, z, p) * scale_ref[p, 0:1, :]
        half = flipped.T
        inner = jnp.sum(half * total_s[p, K : K + 1, :], axis=1, keepdims=True)
        mean_weight = jnp.sum(flipped * inner, axis=0, keepdims=True)
        transform = (jnp.sqrt(float(K - 1)) * flipped + mean_weight).astype(BF16)
        if edges:
            rows = states_s.shape[3]
            result = analysed(states_s[:, OUTER[p]].reshape(K, rows), transform)
            whole[:, p] = result.reshape(PEERS, K // PEERS, rows)
        else:
            out_ref[p] = transform
    if edges:
        cut_for_peers(whole, out_refs)
    else:
        add_up(sums_ref, OUTER, 0)


def root_weights(edges, *args):
    n = 2
    piece = pltpu.VMEM((n, K, K), BF16)
    two, full, edge = (pltpu.VMEM(shape, F32) for shape in ((n, EXT, K), (PATCHES, EXT, K), (2, EDGE, K)))
    if edges:
        states = args[-1].shape
        block, twice = (n,) + states[2:], (2 * n,) + states[2:]
        shapes = [jax.ShapeDtypeStruct(shape, BF16) for shape in (block, twice, twice, block, block, block)]
        more = [pltpu.VMEM((PEERS,) + block, BF16), pltpu.VMEM(states, BF16), pltpu.SemaphoreType.DMA((1,))]
    else:
        shapes = [jax.ShapeDtypeStruct((n, K, K), BF16), jax.ShapeDtypeStruct((n, EXT, K), F32)]
        more = []
    return pl.pallas_call(
        functools.partial(root_kernel, edges),
        in_specs=[ANY] * len(args),
        out_specs=[VMEM] * len(shapes),
        out_shape=shapes,
        scratch_shapes=more
        + ([two, edge] if edges else [two, full, full, two])
        + [pltpu.SemaphoreType.DMA((3,))]
        + [piece] * 6
        + [pltpu.VMEM((K, K), F32), pltpu.VMEM((n, 8, K), F32)],
        compiler_params=PARAMS,
        cost_estimate=pl.CostEstimate(flops=ROOT_COST, bytes_accessed=1000, transcendentals=0),
        name="root_weights",
    )(*args)


def apply_kernel(flipped_ref, states, out_ref, states_s, sems):
    rows = states_s.shape[3]
    copies = [pltpu.make_async_copy(states.at[:, p], states_s.at[:, i], sems.at[i]) for i, p in enumerate(INNER)]
    start_all(copies)
    for i, copy in enumerate(copies):
        copy.wait()
        result = analysed(states_s[:, i].reshape(K, rows), flipped_ref[i])
        out_ref[:, i] = result.reshape(PEERS, K // PEERS, rows)


def apply_weights(flipped, states):
    shape = (PEERS, len(INNER)) + states.shape[2:]
    return pl.pallas_call(
        apply_kernel,
        in_specs=[VMEM, ANY],
        out_specs=VMEM,
        out_shape=jax.ShapeDtypeStruct(shape, BF16),
        scratch_shapes=[pltpu.VMEM(shape, BF16), pltpu.SemaphoreType.DMA((PEERS,))],
        compiler_params=SMALL,
        cost_estimate=COST,
        name="apply_weights",
    )(flipped, states)


def place(parts, out, sems):
    me = lax.axis_index("mem")
    copies = []
    for ref, places in parts:
        source = lax.rem(me + PEERS - places, PEERS)
        for i, p in enumerate(OUTER):
            copies.append(pltpu.make_async_copy(ref.at[i], out.at[source, p], sems.at[len(copies)]))
    return copies


def gather_kernel(first, c0, c2, c6, c1, c7, out, sems):
    copies = place(((c0, 0), (c1, 1), (c2, 2), (c6, 6), (c7, 7)), out, sems)
    for j in range(PEERS):
        copies.append(pltpu.make_async_copy(first.at[j], out.at[j, pl.ds(1, 2)], sems.at[len(copies)]))
    start_all(copies)
    for copy in copies:
        copy.wait()


def gather_rest_kernel(so_far, c4, c3, c5, out, sems):
    copies = place(((c4, 4), (c3, 3), (c5, 5)), out, sems)
    start_all(copies)
    for copy in copies:
        copy.wait()


def gather(first, c0, c2, c6, c1, c7, c4, c3, c5):
    shape = jax.ShapeDtypeStruct((PEERS, PATCHES) + first.shape[2:], BF16)
    some = pl.pallas_call(
        gather_kernel,
        in_specs=[VMEM] * 6,
        out_specs=ANY,
        out_shape=shape,
        scratch_shapes=[pltpu.SemaphoreType.DMA((18,))],
        compiler_params=SMALL,
        cost_estimate=COST,
        name="gather",
    )(first, c0, c2, c6, c1, c7)
    return pl.pallas_call(
        gather_rest_kernel,
        in_specs=[ANY] + [VMEM] * 3,
        out_specs=ANY,
        out_shape=shape,
        input_output_aliases={0: 0},
        scratch_shapes=[pltpu.SemaphoreType.DMA((6,))],
        compiler_params=SMALL,
        cost_estimate=COST,
        name="gather_rest",
    )(some, c4, c3, c5)


def swap(value):
    return lax.all_to_all(value, "mem", split_axis=0, concat_axis=0, tiled=True)


def shift(value, axis, by):
    peers = lax.axis_size(axis)
    return lax.ppermute(value, axis, [(i, (i + by) % peers) for i in range(peers)])


def pair(value, axis, first):
    peers = lax.axis_size(axis)
    pairs = [((i + first) % peers, (i + 1 + first) % peers) for i in range(0, peers, 2)]
    return lax.ppermute(value, axis, pairs + [(j, i) for i, j in pairs])


def spread(c0, c2, c6, c1, c7, c4):
    n = c0.shape[0]
    c2 = shift(c2, "mem", 2)
    c6 = shift(c6, "mem", -2)
    c1 = shift(c1, "mem", 1)
    c7 = shift(c7, "mem", -1)
    c4 = shift(c4, "mem", 4)
    c3 = shift(c2[n:], "mem", 1)
    c5 = shift(c6[n:], "mem", -1)
    return c0, c2, c6, c1, c7, c4, c3, c5


def body(background, obs_ensemble, innovation, obs_precision, taper_weight, obs_count):
    rows = background.shape[3]
    background = background.reshape(PEERS, PATCHES, K // PEERS, rows)
    obs = (obs_count.reshape(PATCHES), obs_ensemble, innovation, obs_precision, taper_weight.transpose(0, 2, 1, 3))
    states = swap(background)
    near, far, following, previous = sent_grams(*obs)
    near = pair(near, "reg", 0)
    far = pair(far, "reg", 1)
    following = shift(following, "mem", 1)
    previous = shift(previous, "mem", -1)
    own = kept_grams(*obs)
    flipped, sums = root_weights(False, own, near, far)
    first = apply_weights(flipped, states)
    first, following, previous = lax.optimization_barrier((first, following, previous))
    first = swap(first)
    blocks = root_weights(True, sums, following, previous, states)
    analysis = gather(first, *spread(*blocks))
    return analysis.reshape(1, PEERS * PATCHES, K // PEERS, rows)


def solution(mesh):
    in_specs = (
        P("reg", None, "mem", None),
        P("reg", "mem", None, None),
        P("reg", "mem", None),
        P("reg", "mem", None),
        P("reg", "mem", None, None),
        P("reg", "mem"),
    )
    out_specs = P("reg", None, "mem", None)
    return jax.shard_map(body, mesh=mesh, in_specs=in_specs, out_specs=out_specs, check_vma=False)
```

```python
import functools
import jax
import jax.numpy as jnp
from jax import lax
from jax.experimental import pallas as pl
from jax.experimental.pallas import tpu as pltpu
from jax.sharding import PartitionSpec as P

F32 = jnp.float32
BF16 = jnp.bfloat16
ITERS = 12
ROOT_COST = 2 * 10**9
INNER = (1, 2)
OUTER = (0, 3)
PATCHES = 4
SIDES = 5
K = 256
SLOTS = 2048
PEERS = 8
EXT = K + 8
HALF = K // 2
EDGE = HALF + 8
VMEM = pl.BlockSpec(memory_space=pltpu.VMEM)
SMEM = pl.BlockSpec(memory_space=pltpu.SMEM)
ANY = pl.BlockSpec(memory_space=pl.ANY)
PARAMS = pltpu.CompilerParams(vmem_limit_bytes=24 << 20)
SMALL = pltpu.CompilerParams(vmem_limit_bytes=16 << 20)
COST = pl.CostEstimate(flops=1000, bytes_accessed=1000, transcendentals=0)


def dot(a, b):
    return jnp.dot(a, b, preferred_element_type=F32)


def split(x):
    high = x.astype(BF16)
    return high, (x - high.astype(F32)).astype(BF16)


def start_all(copies):
    for copy in copies:
        copy.start()


def pick_row(value, p):
    patch = lax.broadcasted_iota(jnp.int32, (PATCHES, SLOTS), 0)
    return jnp.sum(jnp.where(patch == p, value.astype(F32), 0.0), axis=0, keepdims=True)


def slot_weights(p, count_ref, prec_ref, taper_ref):
    slot = lax.broadcasted_iota(jnp.int32, (1, SLOTS), 1)
    prec = jnp.where(slot < count_ref[p], pick_row(prec_ref[0], p), 0.0)
    return [prec * pick_row(taper_ref[0, d], p) for d in range(SIDES)]


def weighted_grams(ens_ref, flipped_ref, rows, innov):
    flipped_ref[0:K] = ens_ref[0, 0].T
    flipped_ref[K:] = jnp.broadcast_to(innov, (16, SLOTS)).astype(BF16)
    flipped = flipped_ref[...]
    pairs = []
    for row in rows:
        scaled = (flipped[0:K].astype(F32) * row).astype(BF16)
        both = lax.dot_general(flipped, scaled, (((1,), (1,)), ((), ())), preferred_element_type=F32)
        pairs.append((both[0:K], both[K : K + 1]))
    return pairs


def upper_lower(n):
    row = lax.broadcasted_iota(jnp.int32, (n, n), 0)
    col = lax.broadcasted_iota(jnp.int32, (n, n), 1)
    return row <= col, row == col


def diagonal(gram):
    return jnp.sum(jnp.where(upper_lower(K)[1], gram, 0.0), axis=0, keepdims=True)


def unpacked(packed, diag):
    upper, same = upper_lower(packed.shape[0])
    flipped = packed.T
    return jnp.where(upper, packed, flipped), jnp.where(same, diag, jnp.where(upper, flipped, packed))


def unfolded(ref):
    ahead, behind = unpacked(ref[0:HALF, 0:HALF], ref[HALF + 1 : HALF + 2, HALF:])
    across = ref[0:HALF, HALF:]
    return jnp.concatenate(
        [jnp.concatenate([ahead, across], axis=1), jnp.concatenate([across.T, behind], axis=1)], axis=0
    )


def sent_kernel(count_ref, ens_ref, innov_ref, prec_ref, taper_ref, near_ref, far_ref, next_ref, prev_ref, flipped_ref):
    even = lax.rem(lax.axis_index("reg"), 2) == 0
    for p in range(PATCHES):

        @pl.when(pl.program_id(0) == p)
        def _():
            weights = slot_weights(p, count_ref, prec_ref, taper_ref)
            rows = [jnp.where(even, weights[1], weights[2]), jnp.where(even, weights[2], weights[1])]
            rows += {0: [weights[4]], PATCHES - 1: [weights[3]]}.get(p, [])
            (near, near_drive), (far, far_drive), *edge = weighted_grams(ens_ref, flipped_ref, rows, pick_row(innov_ref[0], p))
            far = 0.5 * (far + far.T)
            near_ref[0, 0:K, :] = near
            near_ref[0, K:EXT, :] = jnp.broadcast_to(near_drive, (EXT - K, K))
            if p < 2:
                far_ref[p, 0:K, :] = far
                far_ref[p, K:EXT, :] = jnp.broadcast_to(far_drive, (EXT - K, K))
            else:
                at = PATCHES - 1 - p
                far_ref[at, 0:K, :] = jnp.where(upper_lower(K)[0], far_ref[at, 0:K, :], far)
                far_ref[at, K + 1 : K + 2, :] = far_drive
                far_ref[at, K + 2 : K + 3, :] = diagonal(far)
            for (gram, drive), ref in zip(edge, (next_ref if p else prev_ref,)):
                gram = 0.5 * (gram + gram.T)
                ref[0, 0:HALF, 0:HALF] = jnp.where(upper_lower(HALF)[0], gram[0:HALF, 0:HALF], gram[HALF:, HALF:])
                ref[0, 0:HALF, HALF:] = gram[0:HALF, HALF:]
                ref[0, HALF:, :] = jnp.broadcast_to(drive, (EDGE - HALF, K))
                ref[0, HALF + 1 : HALF + 2, :] = diagonal(gram)


def kept_kernel(count_ref, ens_ref, innov_ref, prec_ref, taper_ref, own_ref, flipped_ref):
    p = pl.program_id(0)
    weights = slot_weights(p, count_ref, prec_ref, taper_ref)
    innov = pick_row(innov_ref[0], p)

    @pl.when(p == 0)
    def _():
        own_ref[...] = jnp.zeros_like(own_ref)

    def add(sides):
        pairs = weighted_grams(ens_ref, flipped_ref, [weights[d] for d in sides], innov)
        for d, (gram, drive) in zip(sides, pairs):
            to = p + {0: 0, 3: 1, 4: -1}[d]
            own_ref[to, 0:K, :] += gram
            own_ref[to, K : K + 1, :] += drive

    @pl.when(p == 0)
    def _():
        add((0, 3))

    @pl.when((p > 0) & (p < PATCHES - 1))
    def _():
        add((0, 3, 4))

    @pl.when(p == PATCHES - 1)
    def _():
        add((0, 4))


def gram_specs():
    return [
        SMEM,
        pl.BlockSpec((1, 1, SLOTS, K), lambda p: (0, p, 0, 0)),
        pl.BlockSpec((1, PATCHES, SLOTS), lambda p: (0, 0, 0)),
        pl.BlockSpec((1, PATCHES, SLOTS), lambda p: (0, 0, 0)),
        pl.BlockSpec((1, SIDES, PATCHES, SLOTS), lambda p: (0, 0, 0, 0)),
    ]


def sent_grams(*args):
    full = jax.ShapeDtypeStruct((PATCHES, EXT, K), F32)
    two = jax.ShapeDtypeStruct((2, EXT, K), F32)
    one = jax.ShapeDtypeStruct((1, EDGE, K), F32)
    return pl.pallas_call(
        sent_kernel,
        grid=(PATCHES,),
        in_specs=gram_specs(),
        out_specs=[pl.BlockSpec((1, EXT, K), lambda p: (p, 0, 0)), pl.BlockSpec((2, EXT, K), lambda p: (0, 0, 0))]
        + [pl.BlockSpec((1, EDGE, K), lambda p: (0, 0, 0))] * 2,
        out_shape=[full, two, one, one],
        scratch_shapes=[pltpu.VMEM((K + 16, SLOTS), BF16)],
        compiler_params=PARAMS,
        cost_estimate=COST,
        name="sent_grams",
    )(*args)


def kept_grams(*args):
    return pl.pallas_call(
        kept_kernel,
        grid=(PATCHES,),
        in_specs=gram_specs(),
        out_specs=pl.BlockSpec((PATCHES, EXT, K), lambda p: (0, 0, 0)),
        out_shape=jax.ShapeDtypeStruct((PATCHES, EXT, K), F32),
        scratch_shapes=[pltpu.VMEM((K + 16, SLOTS), BF16)],
        compiler_params=PARAMS,
        cost_estimate=COST,
        name="kept_grams",
    )(*args)


def split_to(refs, p, x):
    refs[0][p], refs[1][p] = split(x)


def analysed(states, flipped):
    states = states.astype(F32)
    mean = jnp.sum(states, axis=0, keepdims=True) * (1.0 / K)
    return (mean + dot(flipped, (states - mean).astype(BF16))).astype(BF16)


def cut_for_peers(whole, refs):
    me = lax.axis_index("mem")
    n = whole.shape[1]
    for ref, places in zip(refs, ((0,), (2, 3), (6, 5), (1,), (7,), (4,))):
        for i, away in enumerate(places):
            ref[i * n : (i + 1) * n] = whole[lax.rem(me + away, PEERS)]


def root_kernel(edges, *refs):
    n = 2
    if edges:
        sums, following, previous, states, *refs = refs
        out_refs, (whole, states_s, pert_s, mean_s, state_sem, total_s, edge_s, *rest) = refs[:6], refs[6:]
        fetch = pltpu.make_async_copy(states, states_s, state_sem.at[0])
        sources = [(sums, total_s), (following, edge_s.at[pl.ds(0, 1)]), (previous, edge_s.at[pl.ds(1, 1)])]
    else:
        own, near, far, out_ref, sums_ref, total_s, own_s, near_s, far_s, *rest = refs
        sources = [(own, own_s), (near, near_s), (far, far_s)]
    sems, yh, yl, zh, zl, sh, sl, diag_ref, scale_ref = rest
    y, z, s = (yh, yl), (zh, zl), (sh, sl)
    copies = [pltpu.make_async_copy(a, b, sems.at[i]) for i, (a, b) in enumerate(sources)]
    start_all(copies)
    if edges:
        fetch.start()
    row = lax.broadcasted_iota(jnp.int32, (K, K), 0)
    col = lax.broadcasted_iota(jnp.int32, (K, K), 1)
    diag_ref[...] = jnp.where(row == col, 1.5, 0.0).astype(F32)

    def add_up(ref, patches, pair):
        packed = far_s[pair, 0:K, :]
        for i, (p, gram) in enumerate(zip(patches, unpacked(packed, far_s[pair, K + 2 : K + 3, :]))):
            ref[i, 0:K, :] = own_s[p, 0:K, :] + near_s[p, 0:K, :] + gram
            ref[i, K : K + 1, :] = own_s[p, K : K + 1, :] + near_s[p, K : K + 1, :] + far_s[pair, K + i : K + i + 1, :]

    def product(a, b, p):
        ah, al, bh, bl = a[0][p], a[1][p], b[0][p], b[1][p]
        return dot(jnp.concatenate([ah, ah, al], axis=1), jnp.concatenate([bl, bh, bh], axis=0))

    def residual(p):
        split_to(s, p, diag_ref[...] - 0.5 * product(z, y, p))

    for copy in copies:
        copy.wait()
    if not edges:
        add_up(total_s, INNER, 1)
    for p in range(n):
        if edges:
            total_s[p, 0:K, :] += unfolded(edge_s.at[p])
            total_s[p, K : K + 1, :] += edge_s[p, HALF : HALF + 1, :]
        system = total_s[p, 0:K, :] + jnp.where(row == col, float(K - 1), 0.0)
        bound = jnp.max(jnp.sum(jnp.abs(system), axis=0, keepdims=True), axis=1, keepdims=True)
        scale_ref[p] = jnp.broadcast_to(1.0 / jnp.sqrt(bound), (8, K))
        root = system / bound
        split_to(y, p, root)
        split_to(z, p, diag_ref[...] - 0.5 * root)
    for p in range(n):
        split_to(y, p, product(y, z, p))

    def sweep(index, carry):
        for p in range(n):
            residual(p)
        for p in range(n):
            split_to(y, p, product(y, s, p))
            split_to(z, p, product(s, z, p))
        return carry

    if edges:
        fetch.wait()
        for i, p in enumerate(OUTER):
            value = states_s[:, p].reshape(K, states_s.shape[3]).astype(F32)
            mean_s[i] = jnp.sum(value, axis=0, keepdims=True) * (1.0 / K)
            pert_s[i] = (value - mean_s[i]).astype(BF16)
    lax.fori_loop(0, ITERS - 2, sweep, 0, unroll=True)
    for p in range(n):
        residual(p)
    for p in range(n):
        flipped = product(s, z, p) * scale_ref[p, 0:1, :]
        half = flipped.T
        inner = jnp.sum(half * total_s[p, K : K + 1, :], axis=1, keepdims=True)
        mean_weight = jnp.sum(flipped * inner, axis=0, keepdims=True)
        transform = (jnp.sqrt(float(K - 1)) * flipped + mean_weight).astype(BF16)
        if edges:
            result = (mean_s[p] + dot(transform, pert_s[p])).astype(BF16)
            whole[:, p] = result.reshape(PEERS, K // PEERS, states_s.shape[3])
        else:
            out_ref[p] = transform
    if edges:
        cut_for_peers(whole, out_refs)
    else:
        add_up(sums_ref, OUTER, 0)


def root_weights(edges, *args):
    n = 2
    piece = pltpu.VMEM((n, K, K), BF16)
    two, full, edge = (pltpu.VMEM(shape, F32) for shape in ((n, EXT, K), (PATCHES, EXT, K), (2, EDGE, K)))
    if edges:
        states = args[-1].shape
        block, twice = (n,) + states[2:], (2 * n,) + states[2:]
        shapes = [jax.ShapeDtypeStruct(shape, BF16) for shape in (block, twice, twice, block, block, block)]
        more = [pltpu.VMEM((PEERS,) + block, BF16), pltpu.VMEM(states, BF16)]
        more += [pltpu.VMEM((n, K, states[3]), BF16), pltpu.VMEM((n, 1, states[3]), F32), pltpu.SemaphoreType.DMA((1,))]
    else:
        shapes = [jax.ShapeDtypeStruct((n, K, K), BF16), jax.ShapeDtypeStruct((n, EXT, K), F32)]
        more = []
    return pl.pallas_call(
        functools.partial(root_kernel, edges),
        in_specs=[ANY] * len(args),
        out_specs=[VMEM] * len(shapes),
        out_shape=shapes,
        scratch_shapes=more
        + ([two, edge] if edges else [two, full, full, two])
        + [pltpu.SemaphoreType.DMA((3,))]
        + [piece] * 6
        + [pltpu.VMEM((K, K), F32), pltpu.VMEM((n, 8, K), F32)],
        compiler_params=PARAMS,
        cost_estimate=pl.CostEstimate(flops=ROOT_COST, bytes_accessed=1000, transcendentals=0),
        name="root_weights",
    )(*args)


def apply_kernel(flipped_ref, states, out_ref, states_s, sems):
    rows = states_s.shape[3]
    copies = [pltpu.make_async_copy(states.at[:, p], states_s.at[:, i], sems.at[i]) for i, p in enumerate(INNER)]
    start_all(copies)
    for i, copy in enumerate(copies):
        copy.wait()
        result = analysed(states_s[:, i].reshape(K, rows), flipped_ref[i])
        out_ref[:, i] = result.reshape(PEERS, K // PEERS, rows)


def apply_weights(flipped, states):
    shape = (PEERS, len(INNER)) + states.shape[2:]
    return pl.pallas_call(
        apply_kernel,
        in_specs=[VMEM, ANY],
        out_specs=VMEM,
        out_shape=jax.ShapeDtypeStruct(shape, BF16),
        scratch_shapes=[pltpu.VMEM(shape, BF16), pltpu.SemaphoreType.DMA((PEERS,))],
        compiler_params=SMALL,
        cost_estimate=COST,
        name="apply_weights",
    )(flipped, states)


def place(parts, out, sems):
    me = lax.axis_index("mem")
    copies = []
    for ref, places in parts:
        source = lax.rem(me + PEERS - places, PEERS)
        for i, p in enumerate(OUTER):
            copies.append(pltpu.make_async_copy(ref.at[i], out.at[source, p], sems.at[len(copies)]))
    return copies


def gather_kernel(first, c0, c2, c6, c1, c7, out, sems):
    copies = place(((c0, 0), (c1, 1), (c2, 2), (c6, 6), (c7, 7)), out, sems)
    for j in range(PEERS):
        copies.append(pltpu.make_async_copy(first.at[j], out.at[j, pl.ds(1, 2)], sems.at[len(copies)]))
    start_all(copies)
    for copy in copies:
        copy.wait()


def gather_rest_kernel(so_far, c4, c3, c5, out, sems):
    copies = place(((c4, 4), (c3, 3), (c5, 5)), out, sems)
    start_all(copies)
    for copy in copies:
        copy.wait()


def gather(first, c0, c2, c6, c1, c7, c4, c3, c5):
    shape = jax.ShapeDtypeStruct((PEERS, PATCHES) + first.shape[2:], BF16)
    some = pl.pallas_call(
        gather_kernel,
        in_specs=[VMEM] * 6,
        out_specs=ANY,
        out_shape=shape,
        scratch_shapes=[pltpu.SemaphoreType.DMA((18,))],
        compiler_params=SMALL,
        cost_estimate=COST,
        name="gather",
    )(first, c0, c2, c6, c1, c7)
    return pl.pallas_call(
        gather_rest_kernel,
        in_specs=[ANY] + [VMEM] * 3,
        out_specs=ANY,
        out_shape=shape,
        input_output_aliases={0: 0},
        scratch_shapes=[pltpu.SemaphoreType.DMA((6,))],
        compiler_params=SMALL,
        cost_estimate=COST,
        name="gather_rest",
    )(some, c4, c3, c5)


def swap(value):
    return lax.all_to_all(value, "mem", split_axis=0, concat_axis=0, tiled=True)


def shift(value, axis, by):
    peers = lax.axis_size(axis)
    return lax.ppermute(value, axis, [(i, (i + by) % peers) for i in range(peers)])


def pair(value, axis, first):
    peers = lax.axis_size(axis)
    pairs = [((i + first) % peers, (i + 1 + first) % peers) for i in range(0, peers, 2)]
    return lax.ppermute(value, axis, pairs + [(j, i) for i, j in pairs])


def spread(c0, c2, c6, c1, c7, c4):
    n = c0.shape[0]
    c2 = shift(c2, "mem", 2)
    c6 = shift(c6, "mem", -2)
    c1 = shift(c1, "mem", 1)
    c7 = shift(c7, "mem", -1)
    c4 = shift(c4, "mem", 4)
    c3 = shift(c2[n:], "mem", 1)
    c5 = shift(c6[n:], "mem", -1)
    return c0, c2, c6, c1, c7, c4, c3, c5


def body(background, obs_ensemble, innovation, obs_precision, taper_weight, obs_count):
    rows = background.shape[3]
    background = background.reshape(PEERS, PATCHES, K // PEERS, rows)
    obs = (obs_count.reshape(PATCHES), obs_ensemble, innovation, obs_precision, taper_weight.transpose(0, 2, 1, 3))
    states = swap(background)
    near, far, following, previous = sent_grams(*obs)
    near = pair(near, "reg", 0)
    far = pair(far, "reg", 1)
    following = shift(following, "mem", 1)
    previous = shift(previous, "mem", -1)
    own = kept_grams(*obs)
    flipped, sums = root_weights(False, own, near, far)
    first = apply_weights(flipped, states)
    first, following, previous = lax.optimization_barrier((first, following, previous))
    first = swap(first)
    blocks = root_weights(True, sums, following, previous, states)
    analysis = gather(first, *spread(*blocks))
    return analysis.reshape(1, PEERS * PATCHES, K // PEERS, rows)


def solution(mesh):
    in_specs = (
        P("reg", None, "mem", None),
        P("reg", "mem", None, None),
        P("reg", "mem", None),
        P("reg", "mem", None),
        P("reg", "mem", None, None),
        P("reg", "mem"),
    )
    out_specs = P("reg", None, "mem", None)
    return jax.shard_map(body, mesh=mesh, in_specs=in_specs, out_specs=out_specs, check_vma=False)
```
